256 devices in a mesh: ctx: 32 (over x, y, core), ch: 8 (over z).
Axes of the slice: x: 4, y: 4, z: 8, core: 2. Of those that a mesh axis runs over, the one named last changes fastest.
Arguments:
- projected: bfloat16 [3, 6144, 4096], P(None, 'ctx', 'ch'), may hold values from -6 to 6
- short_filter: float32 [7, 3, 4096], P(None, None, 'ch'), may hold values from -2.5 to 2.5
- medium_filter: bfloat16 [128, 4096], P(None, 'ch'), may hold values from -1.25 to 1.25
- decay: float32 [16, 4096], P(None, 'ch'), may hold values from 3.2552085e-05 to 0.05
- residues: float32 [16, 4096], P(None, 'ch'), may hold values from -3 to 3
- skip_gain: float32 [4096], P('ch'), may hold values from -6 to 6
- out_gain: float32 [4096], P('ch'), may hold values from 0.25 to 1.75
Outputs:
- mixed: bfloat16 [6144, 4096], P('ctx', 'ch')
The draws below stay inside these ranges and needn't reach their ends.
All inputs are finite; a program needn't handle non-finite values.
Results may differ from the reference program's by a relative error of at most 0.014.
Values may be sent and summed in bfloat16 or wider, within the bound.
No kernel may reach another device: no remote copies, remote signals or barrier semaphores. Data moves between devices by JAX's collectives and lax.ppermute only.
A program may use at most 64 MiB of HBM per device.

```python
import math
import jax
import jax.numpy as jnp
from jax import lax

C = 4096
SHORT = 7
MED = 128
MODES = 16
TOKENS = 6144


def draw_medium_filter(key, part):
    key = jax.random.fold_in(key, 7)
    first_key, second_key = jax.random.split(key)
    column = jnp.arange(C).astype(jnp.float32) / C
    spread = jax.random.uniform(second_key, (1, C), jnp.float32)
    base = jnp.clip(jax.random.normal(first_key, (MED, C), jnp.float32), -4.0, 4.0)
    channel_scale = jnp.exp(jnp.log(10.0) * 0.5 * (column[None, :] + spread))
    return (base * channel_scale / (3.0 * jnp.sqrt(float(MED)))).astype(jnp.bfloat16)


def block_scale(stream_key, shape, cuts, least, high):
    gain = 1.0
    for dim, shards_of in cuts:
        draws = jax.random.uniform(jax.random.fold_in(jax.random.fold_in(stream_key, 6), dim), (shards_of,), jnp.float32, least / len(cuts), high / len(cuts))
        gain = gain * jnp.repeat(jnp.exp(draws), shape[dim] // shards_of).reshape((-1,) + (1,) * (len(shape) - 1 - dim))
    return gain


def bell_draw(stream_key, dims, scale, reach, cuts=(), kind=jnp.bfloat16):
    array = jax.random.normal(stream_key, dims, jnp.float32) * scale
    if len(cuts) > 0:
        array = block_scale(stream_key, dims, cuts, -0.22, 0.18) * array
    return jnp.clip(array, min=-reach, max=reach).astype(kind)


def setup_inputs(seed: int = 0) -> dict:
    keys = jax.random.split(jax.random.key(seed), 8)
    projected = bell_draw(keys[0], (3, TOKENS, C), 1.0, 6.0, ((1, 32), (2, 8)))
    short_filter = bell_draw(keys[1], (SHORT, 3, C), 0.4, 2.5, ((2, 8),), jnp.float32)
    medium_filter = draw_medium_filter(jax.random.fold_in(keys[7], 71), 0)
    decay = jnp.clip(jnp.exp(math.log(0.05) - 7.336937 * jax.random.uniform(keys[3], (MODES, C), jnp.float32) ** block_scale(keys[3], (MODES, C), ((1, 8),), -0.2, 0.2)), 3.255208503105678e-05, 0.05)
    residues = bell_draw(keys[4], (MODES, C), 0.5, 3.0, ((1, 8),), jnp.float32)
    skip_gain = bell_draw(keys[5], (C,), 1.0, 6.0, ((0, 8),), jnp.float32)
    out_gain = jnp.clip(1.0 + 0.15 * jax.random.normal(keys[6], (C,), jnp.float32), 0.25, 1.75)
    return {"projected": projected, "short_filter": short_filter, "medium_filter": medium_filter, "decay": decay, "residues": residues, "skip_gain": skip_gain, "out_gain": out_gain}


norm_eps = 1e-06

def causal_taps(series, tap_weights):
    length = series.shape[0]
    padded = jnp.pad(series, ((SHORT - 1, 0), (0, 0)))
    running = jnp.zeros(series.shape, jnp.float32)
    for delay_step in range(SHORT):
        offset_row = SHORT - 1 - delay_step
        running = running + tap_weights[delay_step][None, :] * padded[offset_row:offset_row + length]
    return running

def causal_fft(signal, kernel):
    length = signal.shape[0]
    spectra = jnp.fft.rfft(signal, n=2 * length, axis=0) * jnp.fft.rfft(kernel, n=2 * length, axis=0)
    return jnp.fft.irfft(spectra, n=2 * length, axis=0)[:length]

def reference(projected, short_filter, medium_filter, decay, residues, skip_gain, out_gain):
    group_width = math.gcd(C, 512)
    group_count = C // group_width
    delays = jnp.arange(TOKENS).astype(jnp.float32)[:, None]

    def one_group(group_index):
        first_col = (group_index * group_width).astype(jnp.int32)
        inputs_part = lax.dynamic_slice_in_dim(projected, first_col, group_width, 2).astype(jnp.float32)
        short_part = lax.dynamic_slice_in_dim(short_filter, first_col, group_width, 2)
        featured = jnp.stack([causal_taps(inputs_part[stream_index], short_part[:, stream_index]) for stream_index in range(3)])
        featured = lax.optimization_barrier(featured.astype(jnp.bfloat16)).astype(jnp.float32)
        queries = featured[0]
        product = (featured[1] * featured[2]).astype(jnp.bfloat16)
        medium_part = lax.dynamic_slice_in_dim(medium_filter, first_col, group_width, 1).astype(jnp.float32)
        mediated = causal_fft(product.astype(jnp.float32), medium_part).astype(jnp.bfloat16)
        mediated = lax.optimization_barrier(mediated).astype(jnp.float32)
        decay_rates = lax.dynamic_slice_in_dim(decay, first_col, group_width, 1)
        weights = lax.dynamic_slice_in_dim(residues, first_col, group_width, 1) * jnp.sqrt(-jnp.expm1(-2.0 * decay_rates))
        kernel = jnp.zeros((TOKENS, group_width), jnp.float32)
        for mode_index in range(MODES):
            kernel = kernel + weights[mode_index][None, :] * jnp.exp(-decay_rates[mode_index][None, :] * delays)
        skip_part = lax.dynamic_slice_in_dim(skip_gain, first_col, group_width, 0)
        summed = causal_fft(mediated, kernel) + skip_part[None, :] * mediated
        return queries * summed
    mixed_groups = lax.map(one_group, jnp.arange(group_count).astype(jnp.int32))
    gated_all = jnp.transpose(mixed_groups, (1, 0, 2)).reshape(TOKENS, C)
    mean_square = lax.optimization_barrier(jnp.sum(gated_all * gated_all, axis=1, keepdims=True)) / C
    return (gated_all * lax.rsqrt(mean_square + norm_eps) * out_gain[None, :]).astype(jnp.bfloat16)
```

```python
import functools
import jax
import jax.numpy as jnp
from jax import lax
from jax.experimental import pallas as pl
from jax.experimental.pallas import tpu as pltpu
from jax.sharding import PartitionSpec as P

C = 4096
SHORT = 7
MED = 128
MODES = 16
EPS = 1e-06
LANES = 128
TILE = 8
F32 = jnp.float32
BF16 = jnp.bfloat16
PARAMS = pltpu.CompilerParams(vmem_limit_bytes=48 * 1024 * 1024)


def row_iota():
    return lax.broadcasted_iota(jnp.int32, (TILE, LANES), 0).astype(F32)


def lanes_of(group):
    return pl.ds(pl.multiple_of(group * LANES, LANES), LANES)


def one_minus_exp(x):
    return x * (1 - x * (1 / 2) * (1 - x * (1 / 3) * (1 - x * (1 / 4) * (1 - x * (1 / 5) * (1 - x * (1 / 6))))))


def tiles_of(array):
    return [array[TILE * i : TILE * (i + 1)] for i in range(array.shape[0] // TILE)]


def filter_kernel(med_ref, decay_ref, res_ref, skip_ref, g_ref, wm_ref, med_f32, shifted):
    med_tiles = MED // TILE
    far_tiles = g_ref.shape[0] // TILE - med_tiles

    def group_body(group, _):
        cols = lanes_of(group)
        rows = row_iota()
        decay = decay_ref[:, cols]
        weights = res_ref[:, cols] * jnp.sqrt(one_minus_exp(2.0 * decay))
        eight = jnp.exp(-TILE * decay)
        med = med_ref[:, cols].astype(F32)
        med_f32[...] = med
        near = [jnp.zeros((TILE, LANES), F32) for _ in range(med_tiles)]
        far = [jnp.zeros((TILE, LANES), F32) for _ in range(far_tiles)]
        for n in range(MODES):
            rate = decay[n : n + 1]
            step = jnp.broadcast_to(eight[n : n + 1], (TILE, LANES))
            weight = weights[n : n + 1]
            powers = jnp.exp(-rate * rows)
            term = weight * powers
            state = jnp.zeros((TILE, LANES), F32)
            for i in range(med_tiles):
                near[i] = near[i] + term
                term = term * step
                state = state * step + med[TILE * i : TILE * (i + 1)]
            reach = jnp.sum(state * jnp.exp(-rate * (TILE - 1 - rows)), axis=0, keepdims=True)
            reach = reach * weight
            wm_ref[n : n + 1, cols] = reach
            term = reach * jnp.exp(-rate * (rows + 1))
            for i in range(far_tiles):
                far[i] = far[i] + term
                term = term * step
        near[0] = near[0] + jnp.where(rows == 0, skip_ref[:, cols], 0.0)
        taps = jnp.concatenate(near, 0)
        for s in range(TILE):
            shifted[s, 0:TILE] = jnp.zeros((TILE, LANES), F32)
            shifted[s, s : s + MED] = taps

        def shift_body(s, acc):
            acc = list(acc)
            bank = [shifted[s, TILE * i : TILE * (i + 1)] for i in range(med_tiles)]
            for j in range(med_tiles):
                row = jnp.broadcast_to(med_f32[pl.ds(TILE * j + s, 1), :], (TILE, LANES))
                for i in range(j, med_tiles):
                    acc[i] = acc[i] + row * bank[i - j]
            return tuple(acc)

        acc = lax.fori_loop(0, TILE, shift_body, tuple(jnp.zeros((TILE, LANES), F32) for _ in range(med_tiles)))
        g_ref[:, cols] = jnp.concatenate(list(acc) + far, 0)
        return 0

    lax.fori_loop(0, g_ref.shape[1] // LANES, group_body, 0)


def feature_kernel(proj_ref, halo_ref, short_ref, decay_ref, q_ref, p_ref, tail_ref, spread_ref, ext):
    row_count = proj_ref.shape[1]
    all_tiles = row_count // TILE
    part_tiles = all_tiles - MED // TILE

    def group_body(group, _):
        cols = lanes_of(group)
        rows = row_iota()
        feats = []
        for j in range(3):
            ext[j, 0:TILE] = halo_ref[j, :, cols].astype(F32)[TILE : 2 * TILE]
            ext[j, TILE : TILE + row_count] = proj_ref[j, :, cols].astype(F32)
            total = short_ref[0, j : j + 1, cols] * ext[j, TILE : TILE + row_count]
            for d in range(1, SHORT):
                total = total + short_ref[d, j : j + 1, cols] * ext[j, TILE - d : TILE - d + row_count]
            feats.append(total.astype(BF16))
        q_ref[:, cols] = feats[0]
        product = (feats[1].astype(F32) * feats[2].astype(F32)).astype(BF16)
        p_ref[:, cols] = product
        tail_ref[0:MED, cols] = product[row_count - MED :]
        tiles = tiles_of(product.astype(F32))
        decay = decay_ref[:, cols]
        eight = jnp.exp(-TILE * decay)
        parts, wholes = [], []
        for n in range(MODES):
            step = jnp.broadcast_to(eight[n : n + 1], (TILE, LANES))
            close = jnp.exp(-decay[n : n + 1] * (TILE - 1 - rows))
            state = tiles[0]
            for i in range(1, all_tiles):
                if i == part_tiles:
                    parts.append(jnp.sum(state * close, axis=0, keepdims=True))
                state = state * step + tiles[i]
            wholes.append(jnp.sum(state * close, axis=0, keepdims=True))
        tail_ref[MED : MED + MODES, cols] = jnp.concatenate(parts, 0).astype(BF16)
        whole = jnp.concatenate(wholes, 0).astype(BF16)
        for i in range(spread_ref.shape[0]):
            spread_ref[i, :, cols] = whole
        return 0

    lax.fori_loop(0, q_ref.shape[1] // LANES, group_body, 0)


def mix_kernel(index_ref, g_ref, wm_ref, decay_ref, states_ref, tail_ref, p_ref, q_ref, gated_ref, sums_ref,
               shifted, signal, squares):
    row_count = p_ref.shape[0]
    out_tiles = row_count // TILE
    lead_tiles = MED // TILE
    reach = g_ref.shape[0]
    own = index_ref[0]
    squares[...] = jnp.zeros(squares.shape, F32)

    def group_body(group, _):
        cols = lanes_of(group)
        rows = row_iota()
        for s in range(TILE):
            shifted[s, 0:TILE] = jnp.zeros((TILE, LANES), F32)
            shifted[s, s : s + reach] = g_ref[:, cols]
        tail = tail_ref[:, cols].astype(F32)
        signal[0:MED] = tail[0:MED]
        signal[MED : MED + row_count] = p_ref[:, cols].astype(F32)
        decay = decay_ref[:, cols]
        span = jnp.exp(-float(row_count) * decay)

        def carry_body(j, carried):
            return carried * span + states_ref[j, :, cols].astype(F32)

        carried = lax.fori_loop(0, own - 1, carry_body, jnp.zeros((MODES, LANES), F32))
        carried = tail[MED : MED + MODES] + jnp.exp(-float(row_count - MED) * decay) * carried
        carried = carried * wm_ref[:, cols]
        eight = jnp.exp(-TILE * decay)
        acc = [jnp.zeros((TILE, LANES), F32) for _ in range(out_tiles)]
        for n in range(MODES):
            step = jnp.broadcast_to(eight[n : n + 1], (TILE, LANES))
            term = carried[n : n + 1] * jnp.exp(-decay[n : n + 1] * (rows + 2))
            for i in range(out_tiles):
                acc[i] = acc[i] + term
                term = term * step

        def shift_body(s, acc):
            acc = list(acc)
            for j in range(lead_tiles + out_tiles):
                row = jnp.broadcast_to(signal[pl.ds(TILE * j + s, 1), :], (TILE, LANES))
                for i in range(max(0, j - lead_tiles), out_tiles):
                    off = TILE * (i + lead_tiles - j)
                    acc[i] = acc[i] + row * shifted[s, off : off + TILE]
            return tuple(acc)

        acc = lax.fori_loop(0, TILE, shift_body, tuple(acc))
        gated = jnp.concatenate(acc, 0) * q_ref[:, cols].astype(F32)
        gated_ref[:, cols] = gated
        squares[...] = squares[...] + gated * gated
        return 0

    lax.fori_loop(0, q_ref.shape[1] // LANES, group_body, 0)
    sums = lax.dot_general(
        jnp.ones((TILE, LANES), F32), squares[...], (((1,), (1,)), ((), ())),
        precision=lax.Precision.HIGHEST, preferred_element_type=F32,
    )
    for i in range(sums_ref.shape[0]):
        sums_ref[i] = sums


def norm_kernel(gated_ref, sums_ref, gain_ref, out_ref):
    total = sums_ref[0]
    for i in range(1, sums_ref.shape[0]):
        total = total + sums_ref[i]
    scale = jnp.transpose(lax.rsqrt(total / C + EPS))[:, 0:1]
    out_ref[...] = (gated_ref[...] * scale * gain_ref[...]).astype(BF16)


def shape(dims, dtype):
    return jax.ShapeDtypeStruct(dims, dtype)


def from_behind(block, axis):
    return lax.ppermute(block, axis, [(i - 1, i) for i in range(1, lax.axis_size(axis))])


def on_device(projected, short_filter, medium_filter, decay, residues, skip_gain, out_gain):
    _, row_count, chans = projected.shape
    ctx, ch = lax.axis_size("ctx"), lax.axis_size("ch")
    halo = from_behind(projected[:, row_count - 16 :], "ctx")
    reach = row_count + MED
    taps, reach_weights = pl.pallas_call(
        filter_kernel,
        out_shape=(shape((reach, chans), F32), shape((MODES, chans), F32)),
        scratch_shapes=[pltpu.VMEM((MED, LANES), F32), pltpu.VMEM((TILE, MED + TILE, LANES), F32)],
        compiler_params=PARAMS,
        name="filters",
    )(medium_filter, decay, residues, skip_gain[None])
    queries, product, tail, spread = pl.pallas_call(
        feature_kernel,
        out_shape=(
            shape((row_count, chans), BF16),
            shape((row_count, chans), BF16),
            shape((MED + MODES, chans), BF16),
            shape((ctx, MODES, chans), BF16),
        ),
        scratch_shapes=[pltpu.VMEM((3, row_count + TILE, LANES), F32)],
        compiler_params=PARAMS,
        name="features",
    )(projected, halo, short_filter, decay)
    tail = from_behind(tail, "ctx")
    states = lax.all_to_all(spread, "ctx", 0, 0, tiled=True)
    vmem = pl.BlockSpec(memory_space=pltpu.VMEM)
    gated, sums = pl.pallas_call(
        mix_kernel,
        out_shape=(shape((row_count, chans), F32), shape((ch, TILE, row_count), F32)),
        in_specs=[pl.BlockSpec(memory_space=pltpu.SMEM)] + [vmem] * 7,
        scratch_shapes=[
            pltpu.VMEM((TILE, reach + TILE, LANES), F32),
            pltpu.VMEM((reach, LANES), F32),
            pltpu.VMEM((row_count, LANES), F32),
        ],
        compiler_params=PARAMS,
        name="mix",
    )(lax.axis_index("ctx").reshape(1), taps, reach_weights, decay, states, tail, product, queries)
    sums = lax.all_to_all(sums, "ch", 0, 0, tiled=True)
    return pl.pallas_call(
        norm_kernel,
        out_shape=shape((row_count, chans), BF16),
        compiler_params=PARAMS,
        name="norm",
    )(gated, sums, out_gain[None])


def solution(mesh):
    in_specs = (
        P(None, "ctx", "ch"),
        P(None, None, "ch"),
        P(None, "ch"),
        P(None, "ch"),
        P(None, "ch"),
        P("ch"),
        P("ch"),
    )
    return jax.shard_map(on_device, mesh=mesh, in_specs=in_specs, out_specs=P("ctx", "ch"), check_vma=False)
```

```python
import jax
import jax.numpy as jnp
from jax import lax
from jax.experimental import pallas as pl
from jax.experimental.pallas import tpu as pltpu
from jax.sharding import PartitionSpec as P

C = 4096
SHORT = 7
MED = 128
MODES = 16
EPS = 1e-06
LANES = 128
TILE = 8
F32 = jnp.float32
BF16 = jnp.bfloat16
PARAMS = pltpu.CompilerParams(vmem_limit_bytes=48 * 1024 * 1024)


def row_iota():
    return lax.broadcasted_iota(jnp.int32, (TILE, LANES), 0).astype(F32)


def lanes_of(group):
    return pl.ds(pl.multiple_of(group * LANES, LANES), LANES)


def one_minus_exp(x):
    return x * (1 - x * (1 / 2) * (1 - x * (1 / 3) * (1 - x * (1 / 4) * (1 - x * (1 / 5) * (1 - x * (1 / 6))))))


def tiles_of(array):
    return [array[TILE * i : TILE * (i + 1)] for i in range(array.shape[0] // TILE)]


def filter_kernel(med_ref, decay_ref, res_ref, skip_ref, g_ref, wm_ref, med_f32, shifted):
    med_tiles = MED // TILE
    far_tiles = g_ref.shape[0] // TILE - med_tiles

    def group_body(group, _):
        cols = lanes_of(group)
        rows = row_iota()
        decay = decay_ref[:, cols]
        weights = res_ref[:, cols] * jnp.sqrt(one_minus_exp(2.0 * decay))
        eight = jnp.exp(-TILE * decay)
        med = med_ref[:, cols].astype(F32)
        med_f32[...] = med
        near = [jnp.zeros((TILE, LANES), F32) for _ in range(med_tiles)]
        far = [jnp.zeros((TILE, LANES), F32) for _ in range(far_tiles)]
        for n in range(MODES):
            rate = decay[n : n + 1]
            step = jnp.broadcast_to(eight[n : n + 1], (TILE, LANES))
            weight = weights[n : n + 1]
            powers = jnp.exp(-rate * rows)
            term = weight * powers
            state = jnp.zeros((TILE, LANES), F32)
            for i in range(med_tiles):
                near[i] = near[i] + term
                term = term * step
                state = state * step + med[TILE * i : TILE * (i + 1)]
            reach = jnp.sum(state * jnp.exp(-rate * (TILE - 1 - rows)), axis=0, keepdims=True)
            reach = reach * weight
            wm_ref[n : n + 1, cols] = reach
            term = reach * jnp.exp(-rate * (rows + 1))
            for i in range(far_tiles):
                far[i] = far[i] + term
                term = term * step
        near[0] = near[0] + jnp.where(rows == 0, skip_ref[:, cols], 0.0)
        taps = jnp.concatenate(near, 0)
        for s in range(TILE):
            shifted[s, 0:TILE] = jnp.zeros((TILE, LANES), F32)
            shifted[s, s : s + MED] = taps

        def shift_body(s, acc):
            acc = list(acc)
            bank = [shifted[s, TILE * i : TILE * (i + 1)] for i in range(med_tiles)]
            for j in range(med_tiles):
                row = jnp.broadcast_to(med_f32[pl.ds(TILE * j + s, 1), :], (TILE, LANES))
                for i in range(j, med_tiles):
                    acc[i] = acc[i] + row * bank[i - j]
            return tuple(acc)

        acc = lax.fori_loop(0, TILE, shift_body, tuple(jnp.zeros((TILE, LANES), F32) for _ in range(med_tiles)))
        g_ref[:, cols] = jnp.concatenate(list(acc) + far, 0)
        return 0

    lax.fori_loop(0, g_ref.shape[1] // LANES, group_body, 0)


def feature_kernel(proj_ref, halo_ref, short_ref, decay_ref, after_ref, q_ref, p_ref, tail_ref, spread_ref, ext):
    row_count = proj_ref.shape[1]
    all_tiles = row_count // TILE
    part_tiles = all_tiles - MED // TILE

    def group_body(group, _):
        cols = lanes_of(group)
        rows = row_iota()
        feats = []
        for j in range(3):
            ext[j, 0:TILE] = halo_ref[j, :, cols].astype(F32)[TILE : 2 * TILE]
            ext[j, TILE : TILE + row_count] = proj_ref[j, :, cols].astype(F32)
            total = short_ref[j, 0:1, cols] * ext[j, TILE : TILE + row_count]
            for d in range(1, SHORT):
                total = total + short_ref[j, d : d + 1, cols] * ext[j, TILE - d : TILE - d + row_count]
            feats.append(total.astype(BF16))
        q_ref[:, cols] = feats[0]
        product = (feats[1].astype(F32) * feats[2].astype(F32)).astype(BF16)
        p_ref[:, cols] = product
        tail_ref[0:MED, cols] = product[row_count - MED :]
        tiles = tiles_of(product.astype(F32))
        decay = decay_ref[:, cols]
        eight = jnp.exp(-TILE * decay)
        parts, wholes = [], []
        for n in range(MODES):
            step = jnp.broadcast_to(eight[n : n + 1], (TILE, LANES))
            close = jnp.exp(-decay[n : n + 1] * (TILE - 1 - rows))
            state = tiles[0]
            for i in range(1, all_tiles):
                if i == part_tiles:
                    parts.append(jnp.sum(state * close, axis=0, keepdims=True))
                state = state * step + tiles[i]
            wholes.append(jnp.sum(state * close, axis=0, keepdims=True))
        tail_ref[MED : MED + MODES, cols] = jnp.concatenate(parts, 0).astype(BF16)
        whole = jnp.concatenate(wholes, 0).astype(BF16)
        for i in range(spread_ref.shape[0]):
            spread_ref[i, :, cols] = whole
        return 0

    lax.fori_loop(0, q_ref.shape[1] // LANES, group_body, 0)


def direct_kernel(g_ref, tail_ref, p_ref, near_ref, shifted, signal):
    row_count = p_ref.shape[0]
    out_tiles = row_count // TILE
    lead_tiles = MED // TILE
    reach = g_ref.shape[0]

    def group_body(group, _):
        cols = lanes_of(group)
        for s in range(TILE):
            shifted[s, 0:TILE] = jnp.zeros((TILE, LANES), F32)
            shifted[s, s : s + reach] = g_ref[:, cols]
        signal[0:MED] = tail_ref[0:MED, cols].astype(F32)
        signal[MED : MED + row_count] = p_ref[:, cols].astype(F32)

        def shift_body(s, acc):
            acc = list(acc)
            for j in range(lead_tiles + out_tiles):
                row = jnp.broadcast_to(signal[pl.ds(TILE * j + s, 1), :], (TILE, LANES))
                for i in range(max(0, j - lead_tiles), out_tiles):
                    off = TILE * (i + lead_tiles - j)
                    acc[i] = acc[i] + row * shifted[s, off : off + TILE]
            return tuple(acc)

        acc = lax.fori_loop(0, TILE, shift_body, tuple(jnp.zeros((TILE, LANES), F32) for _ in range(out_tiles)))
        near_ref[:, cols] = jnp.concatenate(acc, 0)
        return 0

    lax.fori_loop(0, p_ref.shape[1] // LANES, group_body, 0)


def combine_kernel(index_ref, wm_ref, decay_ref, states_ref, tail_ref, near_ref, q_ref, gated_ref, sums_ref,
                   entry, squares):
    row_count = q_ref.shape[0]
    out_tiles = row_count // TILE
    squares[...] = jnp.zeros(squares.shape, F32)
    span = jnp.exp(-float(row_count) * decay_ref[...])

    def carry_body(j, carried):
        return carried * span + states_ref[j].astype(F32)

    carried = lax.fori_loop(0, index_ref[0] - 1, carry_body, jnp.zeros(span.shape, F32))
    carried = tail_ref[MED : MED + MODES].astype(F32) + jnp.exp(-float(row_count - MED) * decay_ref[...]) * carried
    entry[...] = carried * wm_ref[...]

    def group_body(group, _):
        cols = lanes_of(group)
        rows = row_iota()
        decay = decay_ref[:, cols]
        eight = jnp.exp(-TILE * decay)
        acc = tiles_of(near_ref[:, cols])
        for n in range(MODES):
            step = jnp.broadcast_to(eight[n : n + 1], (TILE, LANES))
            term = entry[n : n + 1, cols] * jnp.exp(-decay[n : n + 1] * (rows + 2))
            for i in range(out_tiles):
                acc[i] = acc[i] + term
                term = term * step
        gated = jnp.concatenate(acc, 0) * q_ref[:, cols].astype(F32)
        gated_ref[:, cols] = gated
        squares[...] = squares[...] + gated * gated
        return 0

    lax.fori_loop(0, q_ref.shape[1] // LANES, group_body, 0)
    sums = lax.dot_general(
        jnp.ones((TILE, LANES), F32), squares[...], (((1,), (1,)), ((), ())),
        precision=lax.Precision.HIGHEST, preferred_element_type=F32,
    )
    for i in range(sums_ref.shape[0]):
        sums_ref[i] = sums


def norm_kernel(gated_ref, sums_ref, gain_ref, out_ref):
    total = sums_ref[0]
    for i in range(1, sums_ref.shape[0]):
        total = total + sums_ref[i]
    scale = jnp.transpose(lax.rsqrt(total / C + EPS))[:, 0:1]
    out_ref[...] = (gated_ref[...] * scale * gain_ref[...]).astype(BF16)


def shape(dims, dtype):
    return jax.ShapeDtypeStruct(dims, dtype)


def from_behind(block, axis):
    return lax.ppermute(block, axis, [(i - 1, i) for i in range(1, lax.axis_size(axis))])


def on_device(projected, short_filter, medium_filter, decay, residues, skip_gain, out_gain):
    _, row_count, chans = projected.shape
    ctx, ch = lax.axis_size("ctx"), lax.axis_size("ch")
    halo = from_behind(projected[:, row_count - 16 :], "ctx")
    reach = row_count + MED
    vmem = pl.BlockSpec(memory_space=pltpu.VMEM)
    taps, reach_weights = pl.pallas_call(
        filter_kernel,
        out_shape=(shape((reach, chans), F32), shape((MODES, chans), F32)),
        scratch_shapes=[pltpu.VMEM((MED, LANES), F32), pltpu.VMEM((TILE, MED + TILE, LANES), F32)],
        compiler_params=PARAMS,
        name="filters",
    )(medium_filter, decay, residues, skip_gain[None])
    queries, product, tail, spread = pl.pallas_call(
        feature_kernel,
        out_shape=(
            shape((row_count, chans), BF16),
            shape((row_count, chans), BF16),
            shape((MED + MODES, chans), BF16),
            shape((ctx, MODES, chans), BF16),
        ),
        in_specs=[vmem] * 4 + [pl.BlockSpec(memory_space=pl.ANY)],
        scratch_shapes=[pltpu.VMEM((3, row_count + TILE, LANES), F32)],
        compiler_params=PARAMS,
        name="features",
    )(projected, halo, jnp.transpose(short_filter, (1, 0, 2)), decay, reach_weights)
    tail = from_behind(tail, "ctx")
    states = lax.all_to_all(spread, "ctx", 0, 0, tiled=True)
    near = pl.pallas_call(
        direct_kernel,
        out_shape=shape((row_count, chans), F32),
        scratch_shapes=[pltpu.VMEM((TILE, reach + TILE, LANES), F32), pltpu.VMEM((reach, LANES), F32)],
        compiler_params=PARAMS,
        name="direct",
    )(taps, tail, product)
    gated, sums = pl.pallas_call(
        combine_kernel,
        out_shape=(shape((row_count, chans), F32), shape((ch, TILE, row_count), F32)),
        in_specs=[pl.BlockSpec(memory_space=pltpu.SMEM)] + [vmem] * 6,
        scratch_shapes=[pltpu.VMEM((MODES, chans), F32), pltpu.VMEM((row_count, LANES), F32)],
        compiler_params=PARAMS,
        name="combine",
    )(lax.axis_index("ctx").reshape(1), reach_weights, decay, states, tail, near, queries)
    sums = lax.all_to_all(sums, "ch", 0, 0, tiled=True)
    return pl.pallas_call(
        norm_kernel,
        out_shape=shape((row_count, chans), BF16),
        compiler_params=PARAMS,
        name="norm",
    )(gated, sums, out_gain[None])


def solution(mesh):
    in_specs = (
        P(None, "ctx", "ch"),
        P(None, None, "ch"),
        P(None, "ch"),
        P(None, "ch"),
        P(None, "ch"),
        P("ch"),
        P("ch"),
    )
    return jax.shard_map(on_device, mesh=mesh, in_specs=in_specs, out_specs=P("ctx", "ch"), check_vma=False)
```

```python
import functools
import jax
import jax.numpy as jnp
from jax import lax
from jax.experimental import pallas as pl
from jax.experimental.pallas import tpu as pltpu
from jax.sharding import PartitionSpec as P

C = 4096
SHORT = 7
MED = 128
MODES = 16
EPS = 1e-06
LANES = 128
TILE = 8
EDGE = 16
BLOCK = 64
F32 = jnp.float32
BF16 = jnp.bfloat16
PARAMS = pltpu.CompilerParams(vmem_limit_bytes=48 * 1024 * 1024)


def row_iota():
    return lax.broadcasted_iota(jnp.int32, (TILE, LANES), 0).astype(F32)


def lanes_of(group):
    return pl.ds(pl.multiple_of(group * LANES, LANES), LANES)


def one_minus_exp(x):
    return x * (1 - x * (1 / 2) * (1 - x * (1 / 3) * (1 - x * (1 / 4) * (1 - x * (1 / 5) * (1 - x * (1 / 6))))))


def tiles_of(array):
    return [array[TILE * i : TILE * (i + 1)] for i in range(array.shape[0] // TILE)]


def modal_sums(tiles, decay, rows):
    eight = jnp.exp(-TILE * decay)
    sums = []
    for n in range(MODES):
        step = jnp.broadcast_to(eight[n : n + 1], (TILE, LANES))
        state = tiles[0]
        for tile in tiles[1:]:
            state = state * step + tile
        sums.append(jnp.sum(state * jnp.exp(-decay[n : n + 1] * (TILE - 1 - rows)), axis=0, keepdims=True))
    return jnp.concatenate(sums, 0)


def feature_kernel(proj_ref, short_ref, *refs):
    params, (q_ref, p_ref, edge_ref, head_ref), copies, (ext,) = refs[:5], refs[5:9], refs[9:14], refs[14:]
    row_count = proj_ref.shape[1]

    def group_body(group, _):
        cols = lanes_of(group)
        feats = []
        for j in range(3):
            raw = proj_ref[j, :, cols]
            edge_ref[EDGE * j : EDGE * (j + 1), cols] = raw[row_count - EDGE :]
            ext[j, 0:TILE] = jnp.zeros((TILE, LANES), F32)
            ext[j, TILE : TILE + row_count] = raw.astype(F32)
            total = short_ref[j, 0:1, cols] * ext[j, TILE : TILE + row_count]
            for d in range(1, SHORT):
                total = total + short_ref[j, d : d + 1, cols] * ext[j, TILE - d : TILE - d + row_count]
            head_ref[j, :, cols] = total[0:TILE]
            feats.append(total.astype(BF16))
        q_ref[:, cols] = feats[0]
        product = (feats[1].astype(F32) * feats[2].astype(F32)).astype(BF16)
        p_ref[:, cols] = product
        edge_ref[3 * EDGE : 3 * EDGE + MED, cols] = product[row_count - MED :]
        return 0

    lax.fori_loop(0, q_ref.shape[1] // LANES, group_body, 0)
    for param, copied in zip(params, copies):
        copied[...] = param[...]


def table_kernel(p_ref, med_ref, decay_ref, res_ref, skip_ref, g_ref, wm_ref, sums_ref, med_f32, shifted):
    med_tiles = MED // TILE
    far_tiles = g_ref.shape[0] // TILE - med_tiles
    part_tiles = (p_ref.shape[0] - MED) // TILE

    def group_body(group, _):
        cols = lanes_of(group)
        rows = row_iota()
        decay = decay_ref[:, cols]
        weights = res_ref[:, cols] * jnp.sqrt(one_minus_exp(2.0 * decay))
        eight = jnp.exp(-TILE * decay)
        med = med_ref[:, cols].astype(F32)
        med_f32[...] = med
        product = tiles_of(p_ref[:, cols].astype(F32))
        near = [jnp.zeros((TILE, LANES), F32) for _ in range(med_tiles)]
        far = [jnp.zeros((TILE, LANES), F32) for _ in range(far_tiles)]
        for n in range(MODES):
            rate = decay[n : n + 1]
            step = jnp.broadcast_to(eight[n : n + 1], (TILE, LANES))
            weight = weights[n : n + 1]
            powers = jnp.exp(-rate * rows)
            close = jnp.exp(-rate * (TILE - 1 - rows))
            term = weight * powers
            state = jnp.zeros((TILE, LANES), F32)
            for i in range(med_tiles):
                near[i] = near[i] + term
                term = term * step
                state = state * step + med[TILE * i : TILE * (i + 1)]
            reach = jnp.sum(state * close, axis=0, keepdims=True) * weight
            wm_ref[n : n + 1, cols] = reach
            term = reach * jnp.exp(-rate * (rows + 1))
            for i in range(far_tiles):
                far[i] = far[i] + term
                term = term * step
            state = product[1]
            for i in range(2, len(product)):
                if i == part_tiles:
                    sums_ref[1, n : n + 1, cols] = jnp.sum(state * close, axis=0, keepdims=True)
                state = state * step + product[i]
            sums_ref[0, n : n + 1, cols] = jnp.sum(state * close, axis=0, keepdims=True)
        near[0] = near[0] + jnp.where(rows == 0, skip_ref[:, cols], 0.0)
        taps = jnp.concatenate(near, 0)
        for s in range(TILE):
            shifted[s, 0:TILE] = jnp.zeros((TILE, LANES), F32)
            shifted[s, s : s + MED] = taps

        def shift_body(s, acc):
            acc = list(acc)
            bank = [shifted[s, TILE * i : TILE * (i + 1)] for i in range(med_tiles)]
            for j in range(med_tiles):
                row = jnp.broadcast_to(med_f32[pl.ds(TILE * j + s, 1), :], (TILE, LANES))
                for i in range(j, med_tiles):
                    acc[i] = acc[i] + row * bank[i - j]
            return tuple(acc)

        acc = lax.fori_loop(0, TILE, shift_body, tuple(jnp.zeros((TILE, LANES), F32) for _ in range(med_tiles)))
        g_ref[:, cols] = jnp.concatenate(list(acc) + far, 0)
        return 0

    lax.fori_loop(0, g_ref.shape[1] // LANES, group_body, 0)


def first_kernel(edge_ref, head_ref, short_ref, decay_ref, sums_ref, spread_ref, part_ref, first_ref, ext, *, row_count):
    def group_body(group, _):
        cols = lanes_of(group)
        feats = []
        for j in range(3):
            before = edge_ref[EDGE * j : EDGE * (j + 1), cols].astype(F32)
            ext[j, 0:TILE] = before[EDGE - TILE :]
            ext[j, TILE : 2 * TILE] = jnp.zeros((TILE, LANES), F32)
            total = head_ref[j, :, cols]
            for d in range(1, SHORT):
                total = total + short_ref[j, d : d + 1, cols] * ext[j, TILE - d : 2 * TILE - d]
            feats.append(total.astype(BF16).astype(F32))
        product = (feats[1] * feats[2]).astype(BF16).astype(F32)
        first_ref[0, :, cols] = feats[0]
        first_ref[1, :, cols] = product
        decay = decay_ref[:, cols]
        own = modal_sums([product], decay, row_iota())
        whole = sums_ref[0, :, cols] + own * jnp.exp(-float(row_count - TILE) * decay)
        part = sums_ref[1, :, cols] + own * jnp.exp(-float(row_count - MED - TILE) * decay)
        part_ref[:, cols] = part.astype(BF16)
        whole = whole.astype(BF16)
        for i in range(spread_ref.shape[0]):
            spread_ref[i, :, cols] = whole
        return 0

    lax.fori_loop(0, part_ref.shape[1] // LANES, group_body, 0)


def direct_kernel(g_ref, edge_ref, p_ref, first_ref, decay_ref, near_ref, sums_ref, shifted, signal):
    row_count = p_ref.shape[0]
    out_tiles = row_count // TILE
    lead_tiles = MED // TILE
    block_tiles = BLOCK // TILE
    reach = g_ref.shape[0]

    def group_body(group, _):
        cols = lanes_of(group)
        for s in range(TILE):
            shifted[s, 0:TILE] = jnp.zeros((TILE, LANES), F32)
            shifted[s, s : s + reach] = g_ref[:, cols]
        lead = edge_ref[3 * EDGE : 3 * EDGE + MED, cols].astype(F32)
        signal[0:MED] = lead
        signal[MED : MED + row_count] = p_ref[:, cols].astype(F32)
        signal[MED : MED + TILE] = first_ref[1, :, cols]
        for b in range(sums_ref.shape[0]):
            tiles = tiles_of(lead[BLOCK * b : BLOCK * (b + 1)])
            sums_ref[b, :, cols] = modal_sums(tiles, decay_ref[:, cols], row_iota())

        def shift_body(s, acc):
            acc = list(acc)
            for j in range(lead_tiles + out_tiles):
                row = jnp.broadcast_to(signal[pl.ds(TILE * j + s, 1), :], (TILE, LANES))
                for i in range(max(0, j - lead_tiles), min(out_tiles, (j // block_tiles + 1) * block_tiles)):
                    off = TILE * (i + lead_tiles - j)
                    acc[i] = acc[i] + row * shifted[s, off : off + TILE]
            return tuple(acc)

        acc = lax.fori_loop(0, TILE, shift_body, tuple(jnp.zeros((TILE, LANES), F32) for _ in range(out_tiles)))
        near_ref[:, cols] = jnp.concatenate(acc, 0)
        return 0

    lax.fori_loop(0, p_ref.shape[1] // LANES, group_body, 0)


def combine_kernel(index_ref, wm_ref, decay_ref, states_ref, part_ref, lead_ref, near_ref, q_ref, first_ref, gain_ref,
                   gated_ref, sums_ref, entry, squares):
    row_count = q_ref.shape[0]
    block_tiles = BLOCK // TILE
    squares[...] = jnp.zeros(squares.shape, F32)
    span = jnp.exp(-float(row_count) * decay_ref[...])
    block_span = jnp.exp(-float(BLOCK) * decay_ref[...])

    def carry_body(j, carried):
        return carried * span + states_ref[j].astype(F32)

    carried = lax.fori_loop(0, index_ref[0] - 1, carry_body, jnp.zeros(span.shape, F32))
    state = part_ref[...].astype(F32) + jnp.exp(-float(row_count - MED) * decay_ref[...]) * carried
    for b in range(entry.shape[0]):
        entry[b] = state * wm_ref[...]
        if b < lead_ref.shape[0]:
            state = state * block_span + lead_ref[b]

    def group_body(group, _):
        cols = lanes_of(group)
        rows = row_iota()
        decay = decay_ref[:, cols]
        eight = jnp.exp(-TILE * decay)
        acc = tiles_of(near_ref[:, cols])
        for n in range(MODES):
            step = jnp.broadcast_to(eight[n : n + 1], (TILE, LANES))
            powers = jnp.exp(-decay[n : n + 1] * (rows + 2))
            terms = [entry[b, n : n + 1, cols] * powers for b in range(entry.shape[0])]
            for i in range(block_tiles):
                for b in range(entry.shape[0]):
                    acc[b * block_tiles + i] = acc[b * block_tiles + i] + terms[b]
                    if i < block_tiles - 1:
                        terms[b] = terms[b] * step
        query = q_ref[:, cols].astype(F32)
        gated = jnp.concatenate(acc, 0) * jnp.concatenate([first_ref[0, :, cols], query[TILE:]], 0)
        gated_ref[:, cols] = gated * gain_ref[:, cols]
        squares[...] = squares[...] + gated * gated
        return 0

    lax.fori_loop(0, q_ref.shape[1] // LANES, group_body, 0)
    sums = lax.dot_general(
        jnp.ones((TILE, LANES), F32), squares[...], (((1,), (1,)), ((), ())),
        precision=lax.Precision.HIGHEST, preferred_element_type=F32,
    )
    for i in range(sums_ref.shape[0]):
        sums_ref[i] = sums


def norm_kernel(gated_ref, sums_ref, out_ref):
    total = sums_ref[0]
    for i in range(1, sums_ref.shape[0]):
        total = total + sums_ref[i]
    scale = jnp.transpose(lax.rsqrt(total / C + EPS))[:, 0:1]
    out_ref[...] = (gated_ref[...] * scale).astype(BF16)


def shape(dims, dtype):
    return jax.ShapeDtypeStruct(dims, dtype)


def from_behind(block, axis):
    return lax.ppermute(block, axis, [(i - 1, i) for i in range(1, lax.axis_size(axis))])


def shape(dims, dtype=F32):
    return jax.ShapeDtypeStruct(dims, dtype)


def call(kernel, name, out_shape, scratch, args, scalars=0):
    vmem, smem = (pl.BlockSpec(memory_space=space) for space in (pltpu.VMEM, pltpu.SMEM))
    return pl.pallas_call(
        kernel,
        out_shape=out_shape,
        in_specs=[smem] * scalars + [vmem] * (len(args) - scalars),
        out_specs=jax.tree.map(lambda _: vmem, out_shape),
        scratch_shapes=[pltpu.VMEM(dims, F32) for dims in scratch],
        compiler_params=PARAMS,
        name=name,
    )(*args)


def from_behind(block, axis):
    return lax.ppermute(block, axis, [(i - 1, i) for i in range(1, lax.axis_size(axis))])


def on_device(projected, short_filter, medium_filter, decay, residues, skip_gain, out_gain):
    _, rows, chans = projected.shape
    ctx, ch = lax.axis_size("ctx"), lax.axis_size("ch")
    reach = MED + BLOCK
    short = jnp.transpose(short_filter, (1, 0, 2))
    params = (medium_filter, decay, residues, skip_gain[None], out_gain[None])
    queries, product, edge, head, *params = call(
        feature_kernel,
        "features",
        (
            shape((rows, chans), BF16),
            shape((rows, chans), BF16),
            shape((3 * EDGE + MED, chans), BF16),
            shape((3, TILE, chans)),
        )
        + tuple(shape(p.shape, p.dtype) for p in params),
        [(3, rows + TILE, LANES)],
        (projected, short) + params,
    )
    medium_filter, decay, residues, skip_gain, out_gain = params
    edge = from_behind(edge, "ctx")
    taps, reach_weights, partial = call(
        table_kernel,
        "tables",
        (shape((reach, chans)), shape((MODES, chans)), shape((2, MODES, chans))),
        [(MED, LANES), (TILE, MED + TILE, LANES)],
        (product, medium_filter, decay, residues, skip_gain),
    )
    spread, part, first = call(
        functools.partial(first_kernel, row_count=rows),
        "first",
        (shape((ctx, MODES, chans), BF16), shape((MODES, chans), BF16), shape((2, TILE, chans))),
        [(3, 2 * TILE, LANES)],
        (edge, head, short, decay, partial),
    )
    states = lax.all_to_all(spread, "ctx", 0, 0, tiled=True)
    part = from_behind(part, "ctx")
    near, lead = call(
        direct_kernel,
        "direct",
        (shape((rows, chans)), shape((MED // BLOCK, MODES, chans))),
        [(TILE, reach + TILE, LANES), (MED + rows, LANES)],
        (taps, edge, product, first, decay),
    )
    gated, sums = call(
        combine_kernel,
        "combine",
        (shape((rows, chans)), shape((ch, TILE, rows))),
        [(rows // BLOCK, MODES, chans), (rows, LANES)],
        (lax.axis_index("ctx").reshape(1), reach_weights, decay, states, part, lead, near, queries, first, out_gain),
        scalars=1,
    )
    sums = lax.all_to_all(sums, "ch", 0, 0, tiled=True)
    return pl.pallas_call(
        norm_kernel, out_shape=shape((rows, chans), BF16), compiler_params=PARAMS, name="norm"
    )(gated, sums)


def solution(mesh):
    in_specs = (
        P(None, "ctx", "ch"),
        P(None, None, "ch"),
        P(None, "ch"),
        P(None, "ch"),
        P(None, "ch"),
        P("ch"),
        P("ch"),
    )
    return jax.shard_map(on_device, mesh=mesh, in_specs=in_specs, out_specs=P("ctx", "ch"), check_vma=False)
```

```python
import jax
import jax.numpy as jnp
from jax import lax
from jax.experimental import pallas as pl
from jax.experimental.pallas import tpu as pltpu
from jax.sharding import PartitionSpec as P

C = 4096
SHORT = 7
MED = 128
MODES = 16
EPS = 1e-06
LANES = 128
TILE = 8
EDGE = 16
BLOCK = 64
F32 = jnp.float32
BF16 = jnp.bfloat16
PARAMS = pltpu.CompilerParams(vmem_limit_bytes=48 * 1024 * 1024)


def row_iota():
    return lax.broadcasted_iota(jnp.int32, (TILE, LANES), 0).astype(F32)


def lanes_of(group):
    return pl.ds(pl.multiple_of(group * LANES, LANES), LANES)


def one_minus_exp(x):
    return x * (1 - x * (1 / 2) * (1 - x * (1 / 3) * (1 - x * (1 / 4) * (1 - x * (1 / 5) * (1 - x * (1 / 6))))))


def tiles_of(array):
    return [array[TILE * i : TILE * (i + 1)] for i in range(array.shape[0] // TILE)]


def modal_sums(tiles, decay, rows):
    eight = jnp.exp(-TILE * decay)
    sums = []
    for n in range(MODES):
        step = jnp.broadcast_to(eight[n : n + 1], (TILE, LANES))
        state = tiles[0]
        for tile in tiles[1:]:
            state = state * step + tile
        sums.append(jnp.sum(state * jnp.exp(-decay[n : n + 1] * (TILE - 1 - rows)), axis=0, keepdims=True))
    return jnp.concatenate(sums, 0)


def edge_kernel(proj_ref, edge_ref, raw_ref):
    rows = proj_ref.shape[1]
    edge_ref[...] = proj_ref[1:, rows - EDGE :]
    raw_ref[...] = proj_ref[...]


def short_sum(ext, taps, start, rows, first=0):
    total = 0.0
    for d in range(first, SHORT):
        total = total + taps[d : d + 1] * ext[start - d : start - d + rows]
    return total


def feature_kernel(raw_ref, short_ref, p_ref, tail_ref, head_ref, ext):
    row_count = raw_ref.shape[1]

    def group_body(group, _):
        cols = lanes_of(group)
        feats = []
        for j in range(2):
            ext[j, 0:TILE] = jnp.zeros((TILE, LANES), F32)
            ext[j, TILE:] = raw_ref[1 + j, :, cols].astype(F32)
            total = short_sum(ext.at[j], short_ref[1 + j, :, cols], TILE, row_count)
            head_ref[j, :, cols] = total[0:TILE]
            feats.append(total.astype(BF16).astype(F32))
        product = (feats[0] * feats[1]).astype(BF16)
        p_ref[:, cols] = product
        tail_ref[0:MED, cols] = product[row_count - MED :]
        tail_ref[MED:, cols] = raw_ref[0, row_count - EDGE :, cols]
        return 0

    lax.fori_loop(0, p_ref.shape[1] // LANES, group_body, 0)


def first_kernel(index_ref, halo_ref, head_ref, short_ref, decay_ref, p_ref, spread_ref, first_ref, ext):
    following = jnp.minimum(index_ref[0] + 1, spread_ref.shape[0] - 1)
    part_tiles = (p_ref.shape[0] - MED) // TILE

    def group_body(group, _):
        cols = lanes_of(group)
        feats = []
        for j in range(2):
            ext[group, j, 0:TILE] = halo_ref[j, :, cols].astype(F32)[EDGE - TILE :]
            ext[group, j, TILE:] = jnp.zeros((TILE, LANES), F32)
            total = head_ref[j, :, cols] + short_sum(ext.at[group, j], short_ref[1 + j, :, cols], TILE, TILE, 1)
            feats.append(total.astype(BF16).astype(F32))
        product = (feats[0] * feats[1]).astype(BF16).astype(F32)
        first_ref[:, cols] = product
        tiles = tiles_of(p_ref[:, cols].astype(F32))
        decay = decay_ref[:, cols]
        eight = jnp.exp(-TILE * decay)
        wholes, parts = [], []
        for n in range(MODES):
            step = jnp.broadcast_to(eight[n : n + 1], (TILE, LANES))
            close = jnp.exp(-decay[n : n + 1] * (TILE - 1 - row_iota()))
            state = product
            for i in range(1, len(tiles)):
                if i == part_tiles:
                    parts.append(jnp.sum(state * close, axis=0, keepdims=True))
                state = state * step + tiles[i]
            wholes.append(jnp.sum(state * close, axis=0, keepdims=True))
        whole = jnp.concatenate(wholes, 0).astype(BF16)
        for i in range(spread_ref.shape[0]):
            spread_ref[i, :, cols] = whole
        spread_ref[following, :, cols] = jnp.concatenate(parts, 0).astype(BF16)
        return 0

    lax.fori_loop(0, spread_ref.shape[2] // LANES, group_body, 0, unroll=True)


def row_of(ref, row):
    return jnp.broadcast_to(ref[pl.ds(row, 1), :], (TILE, LANES))


def tile_at(bank, index):
    return bank[TILE * index : TILE * (index + 1)]


def pair_up(signal, pairs):
    half = BLOCK // 2
    for b in range(signal.shape[0] // BLOCK):
        pairs[half * b : half * (b + 1)] = signal[BLOCK * b : BLOCK * b + half] + signal[BLOCK * b + half : BLOCK * (b + 1)]


def no_sums(tiles):
    return tuple(jnp.zeros((TILE, LANES), F32) for _ in range(tiles + tiles // 2))


def with_pairs(acc, tiles):
    half = BLOCK // TILE // 2
    return [acc[i] + acc[tiles + i // (2 * half) * half + i % half] for i in range(tiles)]


def add_block(acc, tiles, out, block, distance, bank, signal, pairs, s):
    full = BLOCK // TILE
    half = full // 2
    base = full * distance
    reach = range(1 - half, half)
    mid = {o: tile_at(bank, base + o) for o in reach}
    upper = {o: tile_at(bank, base + o - half) - mid[o] for o in reach}
    lower = {o: tile_at(bank, base + o + half) - mid[o] for o in reach}
    for j in range(half):
        late = row_of(signal, TILE * (full * block + half + j) + s)
        early = row_of(signal, TILE * (full * block + j) + s)
        both = row_of(pairs, TILE * (half * block + j) + s)
        for i in range(half):
            at = full * out + i
            acc[at] = acc[at] + late * upper[i - j]
            acc[at + half] = acc[at + half] + early * lower[i - j]
            acc[tiles + half * out + i] = acc[tiles + half * out + i] + both * mid[i - j]


def direct_kernel(med_ref, decay_ref, res_ref, skip_ref, gain_ref, short_ref, tail_ref, raw_ref, p_ref, first_ref,
                  q_ref, wm_ref, near_ref, sums_ref, held_ref, med_f32, shifted, signal, pairs, ext):
    row_count = p_ref.shape[0]
    out_tiles = row_count // TILE
    block_tiles = BLOCK // TILE
    blocks = sums_ref.shape[0]
    med_tiles = MED // TILE
    far_tiles = BLOCK // TILE
    reach = MED + BLOCK
    held_ref[...] = gain_ref[...]

    def group_body(group, _):
        cols = lanes_of(group)
        rows = row_iota()
        decay = decay_ref[:, cols]
        weights = res_ref[:, cols] * jnp.sqrt(one_minus_exp(2.0 * decay))
        eight = jnp.exp(-TILE * decay)
        med = med_ref[:, cols].astype(F32)
        med_f32[...] = med
        near = [jnp.zeros((TILE, LANES), F32) for _ in range(med_tiles)]
        far = [jnp.zeros((TILE, LANES), F32) for _ in range(far_tiles)]
        for n in range(MODES):
            rate = decay[n : n + 1]
            step = jnp.broadcast_to(eight[n : n + 1], (TILE, LANES))
            weight = weights[n : n + 1]
            term = weight * jnp.exp(-rate * rows)
            state = jnp.zeros((TILE, LANES), F32)
            for i in range(med_tiles):
                near[i] = near[i] + term
                term = term * step
                state = state * step + med[TILE * i : TILE * (i + 1)]
            reach_weight = jnp.sum(state * jnp.exp(-rate * (TILE - 1 - rows)), axis=0, keepdims=True) * weight
            wm_ref[n : n + 1, cols] = reach_weight
            term = reach_weight * jnp.exp(-rate * (rows + 1))
            for i in range(far_tiles):
                far[i] = far[i] + term
                term = term * step
        near[0] = near[0] + jnp.where(rows == 0, skip_ref[:, cols], 0.0)
        taps = jnp.concatenate(near, 0)
        for s in range(TILE):
            shifted[s, 0:TILE] = jnp.zeros((TILE, LANES), F32)
            shifted[s, s : s + MED] = taps

        def taps_body(s, acc):
            acc = list(acc)
            bank = [shifted[s, TILE * i : TILE * (i + 1)] for i in range(med_tiles)]
            for j in range(med_tiles):
                row = jnp.broadcast_to(med_f32[pl.ds(TILE * j + s, 1), :], (TILE, LANES))
                for i in range(j, med_tiles):
                    acc[i] = acc[i] + row * bank[i - j]
            return tuple(acc)

        acc = lax.fori_loop(0, TILE, taps_body, tuple(jnp.zeros((TILE, LANES), F32) for _ in range(med_tiles)))
        taps = jnp.concatenate(list(acc) + far, 0)
        for s in range(TILE):
            shifted[s, 0:TILE] = jnp.zeros((TILE, LANES), F32)
            shifted[s, s : s + reach] = taps
        tail = tail_ref[:, cols].astype(F32)
        lead = tail[0:MED]
        ext[0:TILE] = tail[MED + EDGE - TILE :]
        ext[TILE:] = raw_ref[0, :, cols].astype(F32)
        q_ref[:, cols] = short_sum(ext, short_ref[0, :, cols], TILE, row_count).astype(BF16)
        signal[0:MED] = lead
        signal[MED : MED + row_count] = p_ref[:, cols].astype(F32)
        signal[MED : MED + TILE] = first_ref[:, cols]
        for b in range(blocks):
            tiles = tiles_of(lead[BLOCK * b : BLOCK * (b + 1)])
            sums_ref[b, :, cols] = modal_sums(tiles, decay, rows)

        pair_up(signal, pairs)

        def direct_body(s, acc):
            bank = shifted.at[s]
            acc = list(acc)
            for j in range(out_tiles):
                row = row_of(signal, MED + TILE * j + s)
                for i in range(j, (j // block_tiles + 1) * block_tiles):
                    acc[i] = acc[i] + row * tile_at(bank, i - j)
            for out in range(out_tiles // block_tiles):
                for distance in range(1, blocks + 1):
                    add_block(acc, out_tiles, out, out + blocks - distance, distance, bank, signal, pairs, s)
            return tuple(acc)

        acc = lax.fori_loop(0, TILE, direct_body, no_sums(out_tiles))
        near_ref[:, cols] = jnp.concatenate(with_pairs(acc, out_tiles), 0)
        return 0

    lax.fori_loop(0, p_ref.shape[1] // LANES, group_body, 0)


def combine_kernel(index_ref, wm_ref, decay_ref, states_ref, lead_ref, near_ref, q_ref, gain_ref,
                   gated_ref, sums_ref, entry, squares):
    row_count = q_ref.shape[0]
    block_tiles = BLOCK // TILE
    own = index_ref[0]
    squares[...] = jnp.zeros(squares.shape, F32)
    span = jnp.exp(-float(row_count) * decay_ref[...])
    block_span = jnp.exp(-float(BLOCK) * decay_ref[...])

    def carry_body(j, carried):
        return carried * span + states_ref[j].astype(F32)

    carried = lax.fori_loop(0, own - 1, carry_body, jnp.zeros(span.shape, F32))
    part = states_ref[jnp.maximum(own - 1, 0)].astype(F32)
    state = jnp.where(own > 0, part, 0.0) + jnp.exp(-float(row_count - MED) * decay_ref[...]) * carried
    for b in range(entry.shape[0]):
        entry[b] = state * wm_ref[...]
        if b < lead_ref.shape[0]:
            state = state * block_span + lead_ref[b]

    def group_body(group, _):
        cols = lanes_of(group)
        rows = row_iota()
        decay = decay_ref[:, cols]
        eight = jnp.exp(-TILE * decay)
        acc = tiles_of(near_ref[:, cols])
        for n in range(MODES):
            step = jnp.broadcast_to(eight[n : n + 1], (TILE, LANES))
            powers = jnp.exp(-decay[n : n + 1] * (rows + 2))
            terms = [entry[b, n : n + 1, cols] * powers for b in range(entry.shape[0])]
            for i in range(block_tiles):
                for b in range(entry.shape[0]):
                    acc[b * block_tiles + i] = acc[b * block_tiles + i] + terms[b]
                    if i < block_tiles - 1:
                        terms[b] = terms[b] * step
        gated = jnp.concatenate(acc, 0) * q_ref[:, cols].astype(F32)
        gated_ref[:, cols] = gated * gain_ref[:, cols]
        squares[...] = squares[...] + gated * gated
        return 0

    lax.fori_loop(0, q_ref.shape[1] // LANES, group_body, 0)
    sums = lax.dot_general(
        jnp.ones((TILE, LANES), F32), squares[...], (((1,), (1,)), ((), ())),
        precision=lax.Precision.HIGHEST, preferred_element_type=F32,
    )
    for i in range(sums_ref.shape[0]):
        sums_ref[i] = sums[0:1]


def norm_kernel(gated_ref, sums_ref, out_ref):
    total = sums_ref[0]
    for i in range(1, sums_ref.shape[0]):
        total = total + sums_ref[i]
    scale = jnp.broadcast_to(lax.rsqrt(total / C + EPS), (TILE, total.shape[1]))
    scale = jnp.transpose(scale)[:, 0:1]
    out_ref[...] = (gated_ref[...] * scale).astype(BF16)


def shape(dims, dtype):
    return jax.ShapeDtypeStruct(dims, dtype)


def cost(flops):
    return pl.CostEstimate(flops=int(flops), bytes_accessed=0, transcendentals=0)


def from_behind(block, axis):
    return lax.ppermute(block, axis, [(i - 1, i) for i in range(1, lax.axis_size(axis))])


def shape(dims, dtype=F32):
    return jax.ShapeDtypeStruct(dims, dtype)


def call(kernel, name, out_shape, scratch, args, scalars=0, cost=None):
    vmem, smem = (pl.BlockSpec(memory_space=space) for space in (pltpu.VMEM, pltpu.SMEM))
    return pl.pallas_call(
        kernel,
        out_shape=out_shape,
        in_specs=[smem] * scalars + [vmem] * (len(args) - scalars),
        out_specs=jax.tree.map(lambda _: vmem, out_shape),
        scratch_shapes=[pltpu.VMEM(dims, F32) for dims in scratch],
        compiler_params=PARAMS,
        cost_estimate=cost,
        name=name,
    )(*args)


def cost(flops):
    return pl.CostEstimate(flops=int(flops), bytes_accessed=0, transcendentals=0)


def from_behind(block, axis):
    return lax.ppermute(block, axis, [(i - 1, i) for i in range(1, lax.axis_size(axis))])


def on_device(projected, short_filter, medium_filter, decay, residues, skip_gain, out_gain):
    _, rows, chans = projected.shape
    ctx, ch = lax.axis_size("ctx"), lax.axis_size("ch")
    index = lax.axis_index("ctx").reshape(1)
    short = jnp.pad(jnp.transpose(short_filter, (1, 0, 2)), ((0, 0), (0, TILE - SHORT), (0, 0)))
    edge, raw = call(
        edge_kernel, "edge", (shape((2, EDGE, chans), BF16), shape(projected.shape, BF16)), [], (projected,)
    )
    halo = from_behind(edge, "ctx")
    product, tail, head = call(
        feature_kernel,
        "features",
        (shape((rows, chans), BF16), shape((MED + EDGE, chans), BF16), shape((2, TILE, chans))),
        [(2, rows + TILE, LANES)],
        (raw, short),
        cost=cost(2e9),
    )
    tail = from_behind(tail, "ctx")
    spread, first = call(
        first_kernel,
        "first",
        (shape((ctx, MODES, chans), BF16), shape((TILE, chans))),
        [(chans // LANES, 2, 2 * TILE, LANES)],
        (index, halo, head, short, decay, product),
        scalars=1,
        cost=cost(2e9),
    )
    states = lax.all_to_all(spread, "ctx", 0, 0, tiled=True)
    queries, reach_weights, near, lead, out_gain = call(
        direct_kernel,
        "direct",
        (
            shape((rows, chans), BF16),
            shape((MODES, chans)),
            shape((rows, chans)),
            shape((MED // BLOCK, MODES, chans)),
            shape((1, chans)),
        ),
        [
            (MED, LANES),
            (TILE, MED + BLOCK + TILE, LANES),
            (MED + rows, LANES),
            ((MED + rows) // 2, LANES),
            (rows + TILE, LANES),
        ],
        (medium_filter, decay, residues, skip_gain[None], out_gain[None], short, tail, raw, product, first),
        cost=cost(8e9),
    )
    gated, sums = call(
        combine_kernel,
        "combine",
        (shape((rows, chans)), shape((ch, 1, rows))),
        [(rows // BLOCK, MODES, chans), (rows, LANES)],
        (index, reach_weights, decay, states, lead, near, queries, out_gain),
        scalars=1,
    )
    sums = lax.all_to_all(sums, "ch", 0, 0, tiled=True)
    return pl.pallas_call(
        norm_kernel, out_shape=shape((rows, chans), BF16), compiler_params=PARAMS, name="norm"
    )(gated, sums)


def solution(mesh):
    in_specs = (
        P(None, "ctx", "ch"),
        P(None, None, "ch"),
        P(None, "ch"),
        P(None, "ch"),
        P(None, "ch"),
        P("ch"),
        P("ch"),
    )
    return jax.shard_map(on_device, mesh=mesh, in_specs=in_specs, out_specs=P("ctx", "ch"), check_vma=False)
```

```python
import jax
import jax.numpy as jnp
from jax import lax
from jax.experimental import pallas as pl
from jax.experimental.pallas import tpu as pltpu
from jax.sharding import PartitionSpec as P

C = 4096
SHORT = 7
MED = 128
MODES = 16
EPS = 1e-06
LANES = 128
TILE = 8
EDGE = 16
BLOCK = 64
F32 = jnp.float32
BF16 = jnp.bfloat16
PARAMS = pltpu.CompilerParams(vmem_limit_bytes=48 * 1024 * 1024)


def row_iota():
    return lax.broadcasted_iota(jnp.int32, (TILE, LANES), 0).astype(F32)


def lanes_of(group):
    return pl.ds(pl.multiple_of(group * LANES, LANES), LANES)


def one_minus_exp(x):
    return x * (1 - x * (1 / 2) * (1 - x * (1 / 3) * (1 - x * (1 / 4) * (1 - x * (1 / 5) * (1 - x * (1 / 6))))))


def tiles_of(array):
    return [array[TILE * i : TILE * (i + 1)] for i in range(array.shape[0] // TILE)]


def modal_sums(tiles, decay, rows):
    eight = jnp.exp(-TILE * decay)
    sums = []
    for n in range(MODES):
        step = jnp.broadcast_to(eight[n : n + 1], (TILE, LANES))
        state = tiles[0]
        for tile in tiles[1:]:
            state = state * step + tile
        sums.append(jnp.sum(state * jnp.exp(-decay[n : n + 1] * (TILE - 1 - rows)), axis=0, keepdims=True))
    return jnp.concatenate(sums, 0)


def edge_kernel(proj_ref, edge_ref, raw_ref):
    rows = proj_ref.shape[1]
    edge_ref[...] = proj_ref[1:, rows - EDGE :]
    raw_ref[...] = proj_ref[...]


def short_sum(ext, taps, start, rows, first=0):
    total = 0.0
    for d in range(first, SHORT):
        total = total + taps[d : d + 1] * ext[start - d : start - d + rows]
    return total


def feature_kernel(raw_ref, short_ref, p_ref, tail_ref, head_ref, ext):
    row_count = raw_ref.shape[1]

    def group_body(group, _):
        cols = lanes_of(group)
        feats = []
        for j in range(2):
            ext[j, 0:TILE] = jnp.zeros((TILE, LANES), F32)
            ext[j, TILE:] = raw_ref[1 + j, :, cols].astype(F32)
            total = short_sum(ext.at[j], short_ref[1 + j, :, cols], TILE, row_count)
            head_ref[j, :, cols] = total[0:TILE]
            feats.append(total.astype(BF16).astype(F32))
        product = (feats[0] * feats[1]).astype(BF16)
        p_ref[:, cols] = product
        tail_ref[0:MED, cols] = product[row_count - MED :]
        tail_ref[MED:, cols] = raw_ref[0, row_count - EDGE :, cols]
        return 0

    lax.fori_loop(0, p_ref.shape[1] // LANES, group_body, 0)


def first_kernel(index_ref, halo_ref, head_ref, short_ref, decay_ref, p_ref, spread_ref, first_ref, ext):
    following = jnp.minimum(index_ref[0] + 1, spread_ref.shape[0] - 1)
    part_tiles = (p_ref.shape[0] - MED) // TILE

    def group_body(group, _):
        cols = lanes_of(group)
        feats = []
        for j in range(2):
            before = halo_ref[j, :, cols].astype(F32)[EDGE - TILE :]
            ext[group, j, 0:TILE] = jnp.where(index_ref[0] > 0, before, 0.0)
            ext[group, j, TILE:] = jnp.zeros((TILE, LANES), F32)
            total = head_ref[j, :, cols] + short_sum(ext.at[group, j], short_ref[1 + j, :, cols], TILE, TILE, 1)
            feats.append(total.astype(BF16).astype(F32))
        product = (feats[0] * feats[1]).astype(BF16).astype(F32)
        first_ref[:, cols] = product
        tiles = tiles_of(p_ref[:, cols].astype(F32))
        decay = decay_ref[:, cols]
        eight = jnp.exp(-TILE * decay)
        wholes, parts = [], []
        for n in range(MODES):
            step = jnp.broadcast_to(eight[n : n + 1], (TILE, LANES))
            close = jnp.exp(-decay[n : n + 1] * (TILE - 1 - row_iota()))
            state = product
            for i in range(1, len(tiles)):
                if i == part_tiles:
                    parts.append(jnp.sum(state * close, axis=0, keepdims=True))
                state = state * step + tiles[i]
            wholes.append(jnp.sum(state * close, axis=0, keepdims=True))
        whole = jnp.concatenate(wholes, 0).astype(BF16)
        for i in range(spread_ref.shape[0]):
            spread_ref[i, :, cols] = whole
        spread_ref[following, :, cols] = jnp.concatenate(parts, 0).astype(BF16)
        return 0

    lax.fori_loop(0, spread_ref.shape[2] // LANES, group_body, 0, unroll=True)


def row_of(ref, row):
    return jnp.broadcast_to(ref[pl.ds(row, 1), :], (TILE, LANES))


def tile_at(bank, index):
    return bank[TILE * index : TILE * (index + 1)]


def pair_up(signal, pairs):
    half = BLOCK // 2
    for b in range(signal.shape[0] // BLOCK):
        pairs[half * b : half * (b + 1)] = signal[BLOCK * b : BLOCK * b + half] + signal[BLOCK * b + half : BLOCK * (b + 1)]


def no_sums(tiles):
    return tuple(jnp.zeros((TILE, LANES), F32) for _ in range(tiles + tiles // 2))


def with_pairs(acc, tiles):
    half = BLOCK // TILE // 2
    return [acc[i] + acc[tiles + i // (2 * half) * half + i % half] for i in range(tiles)]


def add_block(acc, tiles, out, block, distance, bank, signal, pairs, s):
    full = BLOCK // TILE
    half = full // 2
    base = full * distance
    reach = range(1 - half, half)
    mid = {o: tile_at(bank, base + o) for o in reach}
    upper = {o: tile_at(bank, base + o - half) - mid[o] for o in reach}
    lower = {o: tile_at(bank, base + o + half) - mid[o] for o in reach}
    for j in range(half):
        late = row_of(signal, TILE * (full * block + half + j) + s)
        early = row_of(signal, TILE * (full * block + j) + s)
        both = row_of(pairs, TILE * (half * block + j) + s)
        for i in range(half):
            at = full * out + i
            acc[at] = acc[at] + late * upper[i - j]
            acc[at + half] = acc[at + half] + early * lower[i - j]
            acc[tiles + half * out + i] = acc[tiles + half * out + i] + both * mid[i - j]


def direct_kernel(index_ref, med_ref, decay_ref, res_ref, skip_ref, gain_ref, short_ref, tail_ref, raw_ref, p_ref, first_ref,
                  q_ref, base_ref, spans_ref, near_ref, sums_ref, held_ref, med_f32, shifted, signal, pairs, ext):
    row_count = p_ref.shape[0]
    out_tiles = row_count // TILE
    block_tiles = BLOCK // TILE
    blocks = sums_ref.shape[0]
    med_tiles = MED // TILE
    far_tiles = BLOCK // TILE
    reach = MED + BLOCK
    held_ref[...] = gain_ref[...]

    def group_body(group, _):
        cols = lanes_of(group)
        rows = row_iota()
        decay = decay_ref[:, cols]
        weights = res_ref[:, cols] * jnp.sqrt(one_minus_exp(2.0 * decay))
        eight = jnp.exp(-TILE * decay)
        spans_ref[0, :, cols] = jnp.exp(-float(row_count) * decay)
        spans_ref[1, :, cols] = jnp.exp(-float(BLOCK) * decay)
        spans_ref[2, :, cols] = eight
        med = med_ref[:, cols].astype(F32)
        med_f32[...] = med
        near = [jnp.zeros((TILE, LANES), F32) for _ in range(med_tiles)]
        far = [jnp.zeros((TILE, LANES), F32) for _ in range(far_tiles)]
        for n in range(MODES):
            rate = decay[n : n + 1]
            step = jnp.broadcast_to(eight[n : n + 1], (TILE, LANES))
            weight = weights[n : n + 1]
            term = weight * jnp.exp(-rate * rows)
            state = jnp.zeros((TILE, LANES), F32)
            for i in range(med_tiles):
                near[i] = near[i] + term
                term = term * step
                state = state * step + med[TILE * i : TILE * (i + 1)]
            reach_weight = jnp.sum(state * jnp.exp(-rate * (TILE - 1 - rows)), axis=0, keepdims=True) * weight
            base_ref[TILE * n : TILE * (n + 1), cols] = reach_weight * jnp.exp(-rate * (rows + 2))
            term = reach_weight * jnp.exp(-rate * (rows + 1))
            for i in range(far_tiles):
                far[i] = far[i] + term
                term = term * step
        near[0] = near[0] + jnp.where(rows == 0, skip_ref[:, cols], 0.0)
        taps = jnp.concatenate(near, 0)
        for s in range(TILE):
            shifted[s, 0:TILE] = jnp.zeros((TILE, LANES), F32)
            shifted[s, s : s + MED] = taps

        def taps_body(s, acc):
            acc = list(acc)
            bank = [shifted[s, TILE * i : TILE * (i + 1)] for i in range(med_tiles)]
            for j in range(med_tiles):
                row = jnp.broadcast_to(med_f32[pl.ds(TILE * j + s, 1), :], (TILE, LANES))
                for i in range(j, med_tiles):
                    acc[i] = acc[i] + row * bank[i - j]
            return tuple(acc)

        acc = lax.fori_loop(0, TILE, taps_body, tuple(jnp.zeros((TILE, LANES), F32) for _ in range(med_tiles)))
        taps = jnp.concatenate(list(acc) + far, 0)
        for s in range(TILE):
            shifted[s, 0:TILE] = jnp.zeros((TILE, LANES), F32)
            shifted[s, s : s + reach] = taps
        tail = jnp.where(index_ref[0] > 0, tail_ref[:, cols].astype(F32), 0.0)
        lead = tail[0:MED]
        ext[0:TILE] = tail[MED + EDGE - TILE :]
        ext[TILE:] = raw_ref[0, :, cols].astype(F32)
        q_ref[:, cols] = short_sum(ext, short_ref[0, :, cols], TILE, row_count).astype(BF16)
        signal[0:MED] = lead
        signal[MED : MED + row_count] = p_ref[:, cols].astype(F32)
        signal[MED : MED + TILE] = first_ref[:, cols]
        for b in range(blocks):
            tiles = tiles_of(lead[BLOCK * b : BLOCK * (b + 1)])
            sums_ref[b, :, cols] = modal_sums(tiles, decay, rows)

        pair_up(signal, pairs)

        def direct_body(s, acc):
            bank = shifted.at[s]
            acc = list(acc)
            for j in range(out_tiles):
                row = row_of(signal, MED + TILE * j + s)
                for i in range(j, (j // block_tiles + 1) * block_tiles):
                    acc[i] = acc[i] + row * tile_at(bank, i - j)
            for out in range(out_tiles // block_tiles):
                for distance in range(1, blocks + 1):
                    add_block(acc, out_tiles, out, out + blocks - distance, distance, bank, signal, pairs, s)
            return tuple(acc)

        acc = lax.fori_loop(0, TILE, direct_body, no_sums(out_tiles))
        near_ref[:, cols] = jnp.concatenate(with_pairs(acc, out_tiles), 0)
        return 0

    lax.fori_loop(0, p_ref.shape[1] // LANES, group_body, 0)


def combine_kernel(index_ref, base_ref, spans_ref, states_ref, lead_ref, near_ref, q_ref, gain_ref,
                   gated_ref, sums_ref, entry, squares):
    block_tiles = BLOCK // TILE
    own = index_ref[0]
    squares[...] = jnp.zeros(squares.shape, F32)
    span, block_span = spans_ref[0], spans_ref[1]

    def carry_body(j, carried):
        return carried * span + states_ref[j].astype(F32)

    carried = lax.fori_loop(0, own - 1, carry_body, jnp.zeros(span.shape, F32))
    part = states_ref[jnp.maximum(own - 1, 0)].astype(F32)
    state = jnp.where(own > 0, part, 0.0) + block_span * carried
    for b in range(entry.shape[0]):
        entry[b] = state
        if b < lead_ref.shape[0]:
            state = state * block_span + lead_ref[b]

    def group_body(group, _):
        cols = lanes_of(group)
        eight = spans_ref[2, :, cols]
        acc = tiles_of(near_ref[:, cols])
        for n in range(MODES):
            step = jnp.broadcast_to(eight[n : n + 1], (TILE, LANES))
            base = base_ref[TILE * n : TILE * (n + 1), cols]
            terms = [entry[b, n : n + 1, cols] * base for b in range(entry.shape[0])]
            for i in range(block_tiles):
                for b in range(entry.shape[0]):
                    acc[b * block_tiles + i] = acc[b * block_tiles + i] + terms[b]
                    if i < block_tiles - 1:
                        terms[b] = terms[b] * step
        gated = jnp.concatenate(acc, 0) * q_ref[:, cols].astype(F32)
        gated_ref[:, cols] = gated * gain_ref[:, cols]
        squares[...] = squares[...] + gated * gated
        return 0

    lax.fori_loop(0, q_ref.shape[1] // LANES, group_body, 0)
    high = squares[...].astype(BF16)
    low = (squares[...] - high.astype(F32)).astype(BF16)
    sums = lax.dot_general(
        jnp.ones((TILE, 2 * LANES), BF16), jnp.concatenate([high, low], 1), (((1,), (1,)), ((), ())),
        preferred_element_type=F32,
    )
    for i in range(sums_ref.shape[0]):
        sums_ref[i] = sums[0:1]


def norm_kernel(gated_ref, sums_ref, out_ref):
    total = sums_ref[0]
    for i in range(1, sums_ref.shape[0]):
        total = total + sums_ref[i]
    scale = jnp.broadcast_to(lax.rsqrt(total / C + EPS), (TILE, total.shape[1]))
    scale = jnp.transpose(scale)[:, 0:1]
    out_ref[...] = (gated_ref[...] * scale).astype(BF16)


def shape(dims, dtype=F32):
    return jax.ShapeDtypeStruct(dims, dtype)


def call(kernel, name, out_shape, scratch, args, scalars=0, cost=None):
    vmem, smem = (pl.BlockSpec(memory_space=space) for space in (pltpu.VMEM, pltpu.SMEM))
    return pl.pallas_call(
        kernel,
        out_shape=out_shape,
        in_specs=[smem] * scalars + [vmem] * (len(args) - scalars),
        out_specs=jax.tree.map(lambda _: vmem, out_shape),
        scratch_shapes=[pltpu.VMEM(dims, F32) for dims in scratch],
        compiler_params=PARAMS,
        cost_estimate=cost,
        name=name,
    )(*args)


def cost(flops):
    return pl.CostEstimate(flops=int(flops), bytes_accessed=0, transcendentals=0)


def from_behind(block, axis):
    size = lax.axis_size(axis)
    return lax.ppermute(block, axis, [(i, (i + 1) % size) for i in range(size)])


def on_device(projected, short_filter, medium_filter, decay, residues, skip_gain, out_gain):
    _, rows, chans = projected.shape
    ctx, ch = lax.axis_size("ctx"), lax.axis_size("ch")
    index = lax.axis_index("ctx").reshape(1)
    short = jnp.pad(jnp.transpose(short_filter, (1, 0, 2)), ((0, 0), (0, TILE - SHORT), (0, 0)))
    edge, raw = call(
        edge_kernel, "edge", (shape((2, EDGE, chans), BF16), shape(projected.shape, BF16)), [], (projected,)
    )
    halo = from_behind(edge, "ctx")
    product, tail, head = call(
        feature_kernel,
        "features",
        (shape((rows, chans), BF16), shape((MED + EDGE, chans), BF16), shape((2, TILE, chans))),
        [(2, rows + TILE, LANES)],
        (raw, short),
        cost=cost(2e9),
    )
    tail = from_behind(tail, "ctx")
    spread, first = call(
        first_kernel,
        "first",
        (shape((ctx, MODES, chans), BF16), shape((TILE, chans))),
        [(chans // LANES, 2, 2 * TILE, LANES)],
        (index, halo, head, short, decay, product),
        scalars=1,
        cost=cost(2e9),
    )
    states = lax.all_to_all(spread, "ctx", 0, 0, tiled=True)
    queries, base, spans, near, lead, out_gain = call(
        direct_kernel,
        "direct",
        (
            shape((rows, chans), BF16),
            shape((MODES * TILE, chans)),
            shape((3, MODES, chans)),
            shape((rows, chans)),
            shape((MED // BLOCK, MODES, chans)),
            shape((1, chans)),
        ),
        [
            (MED, LANES),
            (TILE, MED + BLOCK + TILE, LANES),
            (MED + rows, LANES),
            ((MED + rows) // 2, LANES),
            (rows + TILE, LANES),
        ],
        (index, medium_filter, decay, residues, skip_gain[None], out_gain[None], short, tail, raw, product, first),
        scalars=1,
        cost=cost(8e9),
    )
    gated, sums = call(
        combine_kernel,
        "combine",
        (shape((rows, chans)), shape((ch, 1, rows))),
        [(rows // BLOCK, MODES, chans), (rows, LANES)],
        (index, base, spans, states, lead, near, queries, out_gain),
        scalars=1,
    )
    sums = lax.all_to_all(sums, "ch", 0, 0, tiled=True)
    return pl.pallas_call(
        norm_kernel, out_shape=shape((rows, chans), BF16), compiler_params=PARAMS, name="norm"
    )(gated, sums)


def solution(mesh):
    in_specs = (
        P(None, "ctx", "ch"),
        P(None, None, "ch"),
        P(None, "ch"),
        P(None, "ch"),
        P(None, "ch"),
        P("ch"),
        P("ch"),
    )
    return jax.shard_map(on_device, mesh=mesh, in_specs=in_specs, out_specs=P("ctx", "ch"), check_vma=False)
```

```python
import functools
import jax
import jax.numpy as jnp
from jax import lax
from jax.experimental import pallas as pl
from jax.experimental.pallas import tpu as pltpu
from jax.sharding import PartitionSpec as P

C = 4096
SHORT = 7
MED = 128
MODES = 16
EPS = 1e-06
LANES = 128
TILE = 8
EDGE = 16
BLOCK = 64
F32 = jnp.float32
BF16 = jnp.bfloat16
PARAMS = pltpu.CompilerParams(vmem_limit_bytes=48 * 1024 * 1024)


def row_iota():
    return lax.broadcasted_iota(jnp.int32, (TILE, LANES), 0).astype(F32)


def lanes_of(group):
    return pl.ds(pl.multiple_of(group * LANES, LANES), LANES)


def one_minus_exp(x):
    return x * (1 - x * (1 / 2) * (1 - x * (1 / 3) * (1 - x * (1 / 4) * (1 - x * (1 / 5) * (1 - x * (1 / 6))))))


def tiles_of(array):
    return [array[TILE * i : TILE * (i + 1)] for i in range(array.shape[0] // TILE)]


def modal_sums(tiles, decay, rows):
    eight = jnp.exp(-TILE * decay)
    sums = []
    for n in range(MODES):
        step = jnp.broadcast_to(eight[n : n + 1], (TILE, LANES))
        state = tiles[0]
        for tile in tiles[1:]:
            state = state * step + tile
        sums.append(jnp.sum(state * jnp.exp(-decay[n : n + 1] * (TILE - 1 - rows)), axis=0, keepdims=True))
    return jnp.concatenate(sums, 0)


def edge_kernel(proj_ref, edge_ref, raw_ref):
    rows = proj_ref.shape[1]
    edge_ref[...] = proj_ref[1:, rows - EDGE :]
    raw_ref[...] = proj_ref[...]


def short_sum(ext, taps, start, rows, first=0):
    total = 0.0
    for d in range(first, SHORT):
        total = total + taps[d : d + 1] * ext[start - d : start - d + rows]
    return total


def feature_kernel(raw_ref, short_ref, p_ref, tail_ref, head_ref, ext):
    row_count = raw_ref.shape[1]

    def group_body(group, _):
        cols = lanes_of(group)
        feats = []
        for j in range(2):
            ext[j, 0:TILE] = jnp.zeros((TILE, LANES), F32)
            ext[j, TILE:] = raw_ref[1 + j, :, cols].astype(F32)
            total = short_sum(ext.at[j], short_ref[1 + j, :, cols], TILE, row_count)
            head_ref[j, :, cols] = total[0:TILE]
            feats.append(total.astype(BF16).astype(F32))
        product = (feats[0] * feats[1]).astype(BF16)
        p_ref[:, cols] = product
        tail_ref[0:MED, cols] = product[row_count - MED :]
        tail_ref[MED:, cols] = raw_ref[0, row_count - EDGE :, cols]
        return 0

    lax.fori_loop(0, p_ref.shape[1] // LANES, group_body, 0)


def state_kernel(p_ref, decay_ref, sums_ref):
    part_tiles = (p_ref.shape[0] - MED) // TILE

    def group_body(group, _):
        cols = lanes_of(group)
        rows = row_iota()
        tiles = tiles_of(p_ref[:, cols].astype(F32))
        decay = decay_ref[:, cols]
        eight = jnp.exp(-TILE * decay)
        for n in range(MODES):
            step = jnp.broadcast_to(eight[n : n + 1], (TILE, LANES))
            close = jnp.exp(-decay[n : n + 1] * (TILE - 1 - rows))
            state = tiles[1]
            for i in range(2, len(tiles)):
                if i == part_tiles:
                    sums_ref[1, n : n + 1, cols] = jnp.sum(state * close, axis=0, keepdims=True)
                state = state * step + tiles[i]
            sums_ref[0, n : n + 1, cols] = jnp.sum(state * close, axis=0, keepdims=True)
        return 0

    lax.fori_loop(0, p_ref.shape[1] // LANES, group_body, 0)


def first_kernel(index_ref, halo_ref, head_ref, short_ref, decay_ref, sums_ref, spread_ref, first_ref, ext, *, row_count):
    following = jnp.minimum(index_ref[0] + 1, spread_ref.shape[0] - 1)

    def group_body(group, _):
        cols = lanes_of(group)
        feats = []
        for j in range(2):
            before = halo_ref[j, :, cols].astype(F32)[EDGE - TILE :]
            ext[group, j, 0:TILE] = jnp.where(index_ref[0] > 0, before, 0.0)
            ext[group, j, TILE:] = jnp.zeros((TILE, LANES), F32)
            total = head_ref[j, :, cols] + short_sum(ext.at[group, j], short_ref[1 + j, :, cols], TILE, TILE, 1)
            feats.append(total.astype(BF16).astype(F32))
        product = (feats[0] * feats[1]).astype(BF16).astype(F32)
        first_ref[:, cols] = product
        decay = decay_ref[:, cols]
        own = modal_sums([product], decay, row_iota())
        whole = sums_ref[0, :, cols] + own * jnp.exp(-float(row_count - TILE) * decay)
        part = sums_ref[1, :, cols] + own * jnp.exp(-float(row_count - MED - TILE) * decay)
        whole = whole.astype(BF16)
        for i in range(spread_ref.shape[0]):
            spread_ref[i, :, cols] = whole
        spread_ref[following, :, cols] = part.astype(BF16)
        return 0

    lax.fori_loop(0, spread_ref.shape[2] // LANES, group_body, 0, unroll=True)


def row_of(ref, row):
    return jnp.broadcast_to(ref[pl.ds(row, 1), :], (TILE, LANES))


def tile_at(bank, index):
    return bank[TILE * index : TILE * (index + 1)]


def pair_up(signal, pairs):
    half = BLOCK // 2
    for b in range(signal.shape[0] // BLOCK):
        pairs[half * b : half * (b + 1)] = signal[BLOCK * b : BLOCK * b + half] + signal[BLOCK * b + half : BLOCK * (b + 1)]


def no_sums(tiles):
    return tuple(jnp.zeros((TILE, LANES), F32) for _ in range(tiles + tiles // 2))


def with_pairs(acc, tiles):
    half = BLOCK // TILE // 2
    return [acc[i] + acc[tiles + i // (2 * half) * half + i % half] for i in range(tiles)]


def add_block(acc, tiles, out, block, distance, bank, signal, pairs, s):
    full = BLOCK // TILE
    half = full // 2
    base = full * distance
    reach = range(1 - half, half)
    mid = {o: tile_at(bank, base + o) for o in reach}
    upper = {o: tile_at(bank, base + o - half) - mid[o] for o in reach}
    lower = {o: tile_at(bank, base + o + half) - mid[o] for o in reach}
    for j in range(half):
        late = row_of(signal, TILE * (full * block + half + j) + s)
        early = row_of(signal, TILE * (full * block + j) + s)
        both = row_of(pairs, TILE * (half * block + j) + s)
        for i in range(half):
            at = full * out + i
            acc[at] = acc[at] + late * upper[i - j]
            acc[at + half] = acc[at + half] + early * lower[i - j]
            acc[tiles + half * out + i] = acc[tiles + half * out + i] + both * mid[i - j]


def direct_kernel(index_ref, med_ref, decay_ref, res_ref, skip_ref, gain_ref, short_ref, tail_ref, raw_ref, p_ref, first_ref,
                  q_ref, base_ref, spans_ref, near_ref, sums_ref, held_ref, med_f32, shifted, signal, pairs, ext):
    row_count = p_ref.shape[0]
    out_tiles = row_count // TILE
    block_tiles = BLOCK // TILE
    blocks = sums_ref.shape[0]
    med_tiles = MED // TILE
    far_tiles = BLOCK // TILE
    reach = MED + BLOCK
    held_ref[...] = gain_ref[...]

    def group_body(group, _):
        cols = lanes_of(group)
        rows = row_iota()
        decay = decay_ref[:, cols]
        weights = res_ref[:, cols] * jnp.sqrt(one_minus_exp(2.0 * decay))
        eight = jnp.exp(-TILE * decay)
        spans_ref[0, :, cols] = jnp.exp(-float(row_count) * decay)
        spans_ref[1, :, cols] = jnp.exp(-float(BLOCK) * decay)
        spans_ref[2, :, cols] = eight
        med = med_ref[:, cols].astype(F32)
        med_f32[...] = med
        near = [jnp.zeros((TILE, LANES), F32) for _ in range(med_tiles)]
        far = [jnp.zeros((TILE, LANES), F32) for _ in range(far_tiles)]
        for n in range(MODES):
            rate = decay[n : n + 1]
            step = jnp.broadcast_to(eight[n : n + 1], (TILE, LANES))
            weight = weights[n : n + 1]
            term = weight * jnp.exp(-rate * rows)
            state = jnp.zeros((TILE, LANES), F32)
            for i in range(med_tiles):
                near[i] = near[i] + term
                term = term * step
                state = state * step + med[TILE * i : TILE * (i + 1)]
            reach_weight = jnp.sum(state * jnp.exp(-rate * (TILE - 1 - rows)), axis=0, keepdims=True) * weight
            base_ref[TILE * n : TILE * (n + 1), cols] = reach_weight * jnp.exp(-rate * (rows + 2))
            term = reach_weight * jnp.exp(-rate * (rows + 1))
            for i in range(far_tiles):
                far[i] = far[i] + term
                term = term * step
        near[0] = near[0] + jnp.where(rows == 0, skip_ref[:, cols], 0.0)
        taps = jnp.concatenate(near, 0)
        for s in range(TILE):
            shifted[s, 0:TILE] = jnp.zeros((TILE, LANES), F32)
            shifted[s, s : s + MED] = taps

        def taps_body(s, acc):
            acc = list(acc)
            bank = [shifted[s, TILE * i : TILE * (i + 1)] for i in range(med_tiles)]
            for j in range(med_tiles):
                row = jnp.broadcast_to(med_f32[pl.ds(TILE * j + s, 1), :], (TILE, LANES))
                for i in range(j, med_tiles):
                    acc[i] = acc[i] + row * bank[i - j]
            return tuple(acc)

        acc = lax.fori_loop(0, TILE, taps_body, tuple(jnp.zeros((TILE, LANES), F32) for _ in range(med_tiles)))
        taps = jnp.concatenate(list(acc) + far, 0)
        for s in range(TILE):
            shifted[s, 0:TILE] = jnp.zeros((TILE, LANES), F32)
            shifted[s, s : s + reach] = taps
        tail = jnp.where(index_ref[0] > 0, tail_ref[:, cols].astype(F32), 0.0)
        lead = tail[0:MED]
        ext[0:TILE] = tail[MED + EDGE - TILE :]
        ext[TILE:] = raw_ref[0, :, cols].astype(F32)
        q_ref[:, cols] = short_sum(ext, short_ref[0, :, cols], TILE, row_count).astype(BF16)
        signal[0:MED] = lead
        signal[MED : MED + row_count] = p_ref[:, cols].astype(F32)
        signal[MED : MED + TILE] = first_ref[:, cols]
        for b in range(blocks):
            tiles = tiles_of(lead[BLOCK * b : BLOCK * (b + 1)])
            sums_ref[b, :, cols] = modal_sums(tiles, decay, rows)

        pair_up(signal, pairs)

        def direct_body(s, acc):
            bank = shifted.at[s]
            acc = list(acc)
            for j in range(out_tiles):
                row = row_of(signal, MED + TILE * j + s)
                for i in range(j, (j // block_tiles + 1) * block_tiles):
                    acc[i] = acc[i] + row * tile_at(bank, i - j)
            for out in range(out_tiles // block_tiles):
                for distance in range(1, blocks + 1):
                    add_block(acc, out_tiles, out, out + blocks - distance, distance, bank, signal, pairs, s)
            return tuple(acc)

        acc = lax.fori_loop(0, TILE, direct_body, no_sums(out_tiles))
        near_ref[:, cols] = jnp.concatenate(with_pairs(acc, out_tiles), 0)
        return 0

    lax.fori_loop(0, p_ref.shape[1] // LANES, group_body, 0)


def combine_kernel(index_ref, base_ref, spans_ref, states_ref, lead_ref, near_ref, q_ref, gain_ref,
                   gated_ref, sums_ref, entry, squares):
    block_tiles = BLOCK // TILE
    own = index_ref[0]
    squares[...] = jnp.zeros(squares.shape, F32)
    span, block_span = spans_ref[0], spans_ref[1]

    def carry_body(j, carried):
        return carried * span + states_ref[j].astype(F32)

    carried = lax.fori_loop(0, own - 1, carry_body, jnp.zeros(span.shape, F32))
    part = states_ref[jnp.maximum(own - 1, 0)].astype(F32)
    state = jnp.where(own > 0, part, 0.0) + block_span * carried
    for b in range(entry.shape[0]):
        entry[b] = state
        if b < lead_ref.shape[0]:
            state = state * block_span + lead_ref[b]

    def group_body(group, _):
        cols = lanes_of(group)
        eight = spans_ref[2, :, cols]
        acc = tiles_of(near_ref[:, cols])
        for n in range(MODES):
            step = jnp.broadcast_to(eight[n : n + 1], (TILE, LANES))
            base = base_ref[TILE * n : TILE * (n + 1), cols]
            terms = [entry[b, n : n + 1, cols] * base for b in range(entry.shape[0])]
            for i in range(block_tiles):
                for b in range(entry.shape[0]):
                    acc[b * block_tiles + i] = acc[b * block_tiles + i] + terms[b]
                    if i < block_tiles - 1:
                        terms[b] = terms[b] * step
        gated = jnp.concatenate(acc, 0) * q_ref[:, cols].astype(F32)
        gated_ref[:, cols] = gated * gain_ref[:, cols]
        squares[...] = squares[...] + gated * gated
        return 0

    lax.fori_loop(0, q_ref.shape[1] // LANES, group_body, 0)
    high = squares[...].astype(BF16)
    low = (squares[...] - high.astype(F32)).astype(BF16)
    sums = lax.dot_general(
        jnp.ones((TILE, 2 * LANES), BF16), jnp.concatenate([high, low], 1), (((1,), (1,)), ((), ())),
        preferred_element_type=F32,
    )
    for i in range(sums_ref.shape[0]):
        sums_ref[i] = sums[0:1]


def norm_kernel(gated_ref, sums_ref, out_ref):
    total = sums_ref[0]
    for i in range(1, sums_ref.shape[0]):
        total = total + sums_ref[i]
    scale = jnp.broadcast_to(lax.rsqrt(total / C + EPS), (TILE, total.shape[1]))
    scale = jnp.transpose(scale)[:, 0:1]
    out_ref[...] = (gated_ref[...] * scale).astype(BF16)


def shape(dims, dtype=F32):
    return jax.ShapeDtypeStruct(dims, dtype)


def call(kernel, name, out_shape, scratch, args, scalars=0, cost=None):
    vmem, smem = (pl.BlockSpec(memory_space=space) for space in (pltpu.VMEM, pltpu.SMEM))
    return pl.pallas_call(
        kernel,
        out_shape=out_shape,
        in_specs=[smem] * scalars + [vmem] * (len(args) - scalars),
        out_specs=jax.tree.map(lambda _: vmem, out_shape),
        scratch_shapes=[pltpu.VMEM(dims, F32) for dims in scratch],
        compiler_params=PARAMS,
        cost_estimate=cost,
        name=name,
    )(*args)


def cost(flops):
    return pl.CostEstimate(flops=int(flops), bytes_accessed=0, transcendentals=0)


def from_behind(block, axis):
    size = lax.axis_size(axis)
    return lax.ppermute(block, axis, [(i, (i + 1) % size) for i in range(size)])


def on_device(projected, short_filter, medium_filter, decay, residues, skip_gain, out_gain):
    _, rows, chans = projected.shape
    ctx, ch = lax.axis_size("ctx"), lax.axis_size("ch")
    index = lax.axis_index("ctx").reshape(1)
    short = jnp.pad(jnp.transpose(short_filter, (1, 0, 2)), ((0, 0), (0, TILE - SHORT), (0, 0)))
    edge, raw = call(
        edge_kernel, "edge", (shape((2, EDGE, chans), BF16), shape(projected.shape, BF16)), [], (projected,)
    )
    halo = from_behind(edge, "ctx")
    product, tail, head = call(
        feature_kernel,
        "features",
        (shape((rows, chans), BF16), shape((MED + EDGE, chans), BF16), shape((2, TILE, chans))),
        [(2, rows + TILE, LANES)],
        (raw, short),
        cost=cost(2e9),
    )
    tail = from_behind(tail, "ctx")
    partial = call(state_kernel, "states", shape((2, MODES, chans)), [], (product, decay), cost=cost(1e9))
    spread, first = call(
        functools.partial(first_kernel, row_count=rows),
        "first",
        (shape((ctx, MODES, chans), BF16), shape((TILE, chans))),
        [(chans // LANES, 2, 2 * TILE, LANES)],
        (index, halo, head, short, decay, partial),
        scalars=1,
        cost=cost(2e9),
    )
    states = lax.all_to_all(spread, "ctx", 0, 0, tiled=True)
    queries, base, spans, near, lead, out_gain = call(
        direct_kernel,
        "direct",
        (
            shape((rows, chans), BF16),
            shape((MODES * TILE, chans)),
            shape((3, MODES, chans)),
            shape((rows, chans)),
            shape((MED // BLOCK, MODES, chans)),
            shape((1, chans)),
        ),
        [
            (MED, LANES),
            (TILE, MED + BLOCK + TILE, LANES),
            (MED + rows, LANES),
            ((MED + rows) // 2, LANES),
            (rows + TILE, LANES),
        ],
        (index, medium_filter, decay, residues, skip_gain[None], out_gain[None], short, tail, raw, product, first),
        scalars=1,
        cost=cost(8e9),
    )
    gated, sums = call(
        combine_kernel,
        "combine",
        (shape((rows, chans)), shape((ch, 1, rows))),
        [(rows // BLOCK, MODES, chans), (rows, LANES)],
        (index, base, spans, states, lead, near, queries, out_gain),
        scalars=1,
    )
    sums = lax.all_to_all(sums, "ch", 0, 0, tiled=True)
    return pl.pallas_call(
        norm_kernel, out_shape=shape((rows, chans), BF16), compiler_params=PARAMS, name="norm"
    )(gated, sums)


def solution(mesh):
    in_specs = (
        P(None, "ctx", "ch"),
        P(None, None, "ch"),
        P(None, "ch"),
        P(None, "ch"),
        P(None, "ch"),
        P("ch"),
        P("ch"),
    )
    return jax.shard_map(on_device, mesh=mesh, in_specs=in_specs, out_specs=P("ctx", "ch"), check_vma=False)
```

```python
import functools
import jax
import jax.numpy as jnp
from jax import lax
from jax.experimental import pallas as pl
from jax.experimental.pallas import tpu as pltpu
from jax.sharding import PartitionSpec as P

C = 4096
SHORT = 7
MED = 128
MODES = 16
EPS = 1e-06
LANES = 128
TILE = 8
EDGE = 16
BLOCK = 64
F32 = jnp.float32
BF16 = jnp.bfloat16
PARAMS = pltpu.CompilerParams(vmem_limit_bytes=48 * 1024 * 1024)


def row_iota():
    return lax.broadcasted_iota(jnp.int32, (TILE, LANES), 0).astype(F32)


def lanes_of(group):
    return pl.ds(pl.multiple_of(group * LANES, LANES), LANES)


def one_minus_exp(x):
    return x * (1 - x * (1 / 2) * (1 - x * (1 / 3) * (1 - x * (1 / 4) * (1 - x * (1 / 5) * (1 - x * (1 / 6))))))


def tiles_of(array):
    return [array[TILE * i : TILE * (i + 1)] for i in range(array.shape[0] // TILE)]


def modal_sums(tiles, decay, rows):
    eight = jnp.exp(-TILE * decay)
    sums = []
    for n in range(MODES):
        step = jnp.broadcast_to(eight[n : n + 1], (TILE, LANES))
        state = tiles[0]
        for tile in tiles[1:]:
            state = state * step + tile
        sums.append(jnp.sum(state * jnp.exp(-decay[n : n + 1] * (TILE - 1 - rows)), axis=0, keepdims=True))
    return jnp.concatenate(sums, 0)


def edge_kernel(proj_ref, edge_ref, raw_ref):
    rows = proj_ref.shape[1]
    edge_ref[...] = proj_ref[1:, rows - EDGE :]
    raw_ref[...] = proj_ref[...]


def short_sum(ext, taps, start, rows, first=0):
    total = 0.0
    for d in range(first, SHORT):
        total = total + taps[d : d + 1] * ext[start - d : start - d + rows]
    return total


def feature_kernel(raw_ref, short_ref, p_ref, tail_ref, head_ref, ext):
    row_count = raw_ref.shape[1]

    def group_body(group, _):
        cols = lanes_of(group)
        feats = []
        for j in range(2):
            ext[j, 0:TILE] = jnp.zeros((TILE, LANES), F32)
            ext[j, TILE:] = raw_ref[1 + j, :, cols].astype(F32)
            total = short_sum(ext.at[j], short_ref[1 + j, :, cols], TILE, row_count)
            head_ref[j, :, cols] = total[0:TILE]
            feats.append(total.astype(BF16).astype(F32))
        product = (feats[0] * feats[1]).astype(BF16)
        p_ref[:, cols] = product
        tail_ref[0:MED, cols] = product[row_count - MED :]
        tail_ref[MED:, cols] = raw_ref[0, row_count - EDGE :, cols]
        return 0

    lax.fori_loop(0, p_ref.shape[1] // LANES, group_body, 0)


def state_kernel(p_ref, decay_ref, sums_ref):
    part_tiles = (p_ref.shape[0] - MED) // TILE

    def group_body(group, _):
        cols = lanes_of(group)
        rows = row_iota()
        tiles = tiles_of(p_ref[:, cols].astype(F32))
        decay = decay_ref[:, cols]
        eight = jnp.exp(-TILE * decay)
        for n in range(MODES):
            step = jnp.broadcast_to(eight[n : n + 1], (TILE, LANES))
            close = jnp.exp(-decay[n : n + 1] * (TILE - 1 - rows))
            state = tiles[1]
            for i in range(2, len(tiles)):
                if i == part_tiles:
                    sums_ref[1, n : n + 1, cols] = jnp.sum(state * close, axis=0, keepdims=True)
                state = state * step + tiles[i]
            sums_ref[0, n : n + 1, cols] = jnp.sum(state * close, axis=0, keepdims=True)
        return 0

    lax.fori_loop(0, p_ref.shape[1] // LANES, group_body, 0)


def first_kernel(index_ref, halo_ref, head_ref, short_ref, decay_ref, sums_ref, spread_ref, first_ref, ext, *, row_count):
    following = jnp.minimum(index_ref[0] + 1, spread_ref.shape[0] - 1)

    def group_body(group, _):
        cols = lanes_of(group)
        feats = []
        for j in range(2):
            before = halo_ref[j, :, cols].astype(F32)[EDGE - TILE :]
            ext[group, j, 0:TILE] = jnp.where(index_ref[0] > 0, before, 0.0)
            ext[group, j, TILE:] = jnp.zeros((TILE, LANES), F32)
            total = head_ref[j, :, cols] + short_sum(ext.at[group, j], short_ref[1 + j, :, cols], TILE, TILE, 1)
            feats.append(total.astype(BF16).astype(F32))
        product = (feats[0] * feats[1]).astype(BF16).astype(F32)
        first_ref[:, cols] = product
        decay = decay_ref[:, cols]
        own = modal_sums([product], decay, row_iota())
        whole = sums_ref[0, :, cols] + own * jnp.exp(-float(row_count - TILE) * decay)
        part = sums_ref[1, :, cols] + own * jnp.exp(-float(row_count - MED - TILE) * decay)
        whole = whole.astype(BF16)
        for i in range(spread_ref.shape[0]):
            spread_ref[i, :, cols] = whole
        spread_ref[following, :, cols] = part.astype(BF16)
        return 0

    lax.fori_loop(0, spread_ref.shape[2] // LANES, group_body, 0, unroll=True)


def row_of(ref, row):
    return jnp.broadcast_to(ref[pl.ds(row, 1), :], (TILE, LANES))


def tile_at(bank, index):
    return bank[TILE * index : TILE * (index + 1)]


def pair_up(signal, pairs):
    half = BLOCK // 2
    for b in range(signal.shape[0] // BLOCK):
        pairs[half * b : half * (b + 1)] = signal[BLOCK * b : BLOCK * b + half] + signal[BLOCK * b + half : BLOCK * (b + 1)]


def no_sums(tiles):
    return tuple(jnp.zeros((TILE, LANES), F32) for _ in range(tiles + tiles // 2))


def with_pairs(acc, tiles):
    half = BLOCK // TILE // 2
    return [acc[i] + acc[tiles + i // (2 * half) * half + i % half] for i in range(tiles)]


def add_block(acc, tiles, out, block, distance, bank, signal, pairs, s):
    full = BLOCK // TILE
    half = full // 2
    base = full * distance
    reach = range(1 - half, half)
    mid = {o: tile_at(bank, base + o) for o in reach}
    upper = {o: tile_at(bank, base + o - half) - mid[o] for o in reach}
    lower = {o: tile_at(bank, base + o + half) - mid[o] for o in reach}
    for j in range(half):
        late = row_of(signal, TILE * (full * block + half + j) + s)
        early = row_of(signal, TILE * (full * block + j) + s)
        both = row_of(pairs, TILE * (half * block + j) + s)
        for i in range(half):
            at = full * out + i
            acc[at] = acc[at] + late * upper[i - j]
            acc[at + half] = acc[at + half] + early * lower[i - j]
            acc[tiles + half * out + i] = acc[tiles + half * out + i] + both * mid[i - j]


def direct_kernel(index_ref, med_ref, decay_ref, res_ref, skip_ref, gain_ref, short_ref, tail_ref, raw_ref, p_ref, first_ref,
                  q_ref, base_ref, spans_ref, near_ref, sums_ref, held_ref, med_f32, shifted, signal, pairs, ext):
    row_count = p_ref.shape[0]
    out_tiles = row_count // TILE
    block_tiles = BLOCK // TILE
    blocks = sums_ref.shape[0]
    med_tiles = MED // TILE
    far_tiles = BLOCK // TILE
    reach = MED + BLOCK
    held_ref[...] = gain_ref[...]

    def group_body(group, _):
        cols = lanes_of(group)
        rows = row_iota()
        decay = decay_ref[:, cols]
        weights = res_ref[:, cols] * jnp.sqrt(one_minus_exp(2.0 * decay))
        eight = jnp.exp(-TILE * decay)
        spans_ref[0, :, cols] = jnp.exp(-float(row_count) * decay)
        spans_ref[1, :, cols] = jnp.exp(-float(BLOCK) * decay)
        spans_ref[2, :, cols] = eight
        med = med_ref[:, cols].astype(F32)
        med_f32[...] = med
        near = [jnp.zeros((TILE, LANES), F32) for _ in range(med_tiles)]
        far = [jnp.zeros((TILE, LANES), F32) for _ in range(far_tiles)]
        for n in range(MODES):
            rate = decay[n : n + 1]
            step = jnp.broadcast_to(eight[n : n + 1], (TILE, LANES))
            weight = weights[n : n + 1]
            term = weight * jnp.exp(-rate * rows)
            state = jnp.zeros((TILE, LANES), F32)
            for i in range(med_tiles):
                near[i] = near[i] + term
                term = term * step
                state = state * step + med[TILE * i : TILE * (i + 1)]
            reach_weight = jnp.sum(state * jnp.exp(-rate * (TILE - 1 - rows)), axis=0, keepdims=True) * weight
            base_ref[TILE * n : TILE * (n + 1), cols] = reach_weight * jnp.exp(-rate * (rows + 2))
            term = reach_weight * jnp.exp(-rate * (rows + 1))
            for i in range(far_tiles):
                far[i] = far[i] + term
                term = term * step
        near[0] = near[0] + jnp.where(rows == 0, skip_ref[:, cols], 0.0)
        taps = jnp.concatenate(near, 0)
        for s in range(TILE):
            shifted[s, 0:TILE] = jnp.zeros((TILE, LANES), F32)
            shifted[s, s : s + MED] = taps

        def taps_body(s, acc):
            acc = list(acc)
            bank = [shifted[s, TILE * i : TILE * (i + 1)] for i in range(med_tiles)]
            for j in range(med_tiles):
                row = jnp.broadcast_to(med_f32[pl.ds(TILE * j + s, 1), :], (TILE, LANES))
                for i in range(j, med_tiles):
                    acc[i] = acc[i] + row * bank[i - j]
            return tuple(acc)

        acc = lax.fori_loop(0, TILE, taps_body, tuple(jnp.zeros((TILE, LANES), F32) for _ in range(med_tiles)))
        taps = jnp.concatenate(list(acc) + far, 0)
        for s in range(TILE):
            shifted[s, 0:TILE] = jnp.zeros((TILE, LANES), F32)
            shifted[s, s : s + reach] = taps
        tail = jnp.where(index_ref[0] > 0, tail_ref[:, cols].astype(F32), 0.0)
        lead = tail[0:MED]
        ext[0:TILE] = tail[MED + EDGE - TILE :]
        ext[TILE:] = raw_ref[0, :, cols].astype(F32)
        q_ref[:, cols] = short_sum(ext, short_ref[0, :, cols], TILE, row_count).astype(BF16)
        signal[0:MED] = lead
        signal[MED : MED + row_count] = p_ref[:, cols].astype(F32)
        signal[MED : MED + TILE] = first_ref[:, cols]
        for b in range(blocks):
            tiles = tiles_of(lead[BLOCK * b : BLOCK * (b + 1)])
            sums_ref[b, :, cols] = modal_sums(tiles, decay, rows)

        pair_up(signal, pairs)

        def direct_body(s, acc):
            bank = shifted.at[s]
            acc = list(acc)
            for j in range(out_tiles):
                row = row_of(signal, MED + TILE * j + s)
                for i in range(j, (j // block_tiles + 1) * block_tiles):
                    acc[i] = acc[i] + row * tile_at(bank, i - j)
            for out in range(out_tiles // block_tiles):
                for distance in range(1, blocks + 1):
                    add_block(acc, out_tiles, out, out + blocks - distance, distance, bank, signal, pairs, s)
            return tuple(acc)

        acc = lax.fori_loop(0, TILE, direct_body, no_sums(out_tiles))
        near_ref[:, cols] = jnp.concatenate(with_pairs(acc, out_tiles), 0)
        return 0

    lax.fori_loop(0, p_ref.shape[1] // LANES, group_body, 0)


def combine_kernel(index_ref, base_ref, spans_ref, states_ref, lead_ref, near_ref, q_ref, gain_ref,
                   gated_ref, sums_ref, entry, squares):
    block_tiles = BLOCK // TILE
    own = index_ref[0]
    squares[...] = jnp.zeros(squares.shape, F32)
    span, block_span = spans_ref[0], spans_ref[1]

    def carry_body(j, carried):
        return carried * span + states_ref[j].astype(F32)

    carried = lax.fori_loop(0, own - 1, carry_body, jnp.zeros(span.shape, F32))
    part = states_ref[jnp.maximum(own - 1, 0)].astype(F32)
    state = jnp.where(own > 0, part, 0.0) + block_span * carried
    for b in range(entry.shape[0]):
        entry[b] = state
        if b < lead_ref.shape[0]:
            state = state * block_span + lead_ref[b]

    def group_body(group, _):
        cols = lanes_of(group)
        eight = spans_ref[2, :, cols]
        acc = tiles_of(near_ref[:, cols])
        for n in range(MODES):
            step = jnp.broadcast_to(eight[n : n + 1], (TILE, LANES))
            base = base_ref[TILE * n : TILE * (n + 1), cols]
            terms = [entry[b, n : n + 1, cols] * base for b in range(entry.shape[0])]
            for i in range(block_tiles):
                for b in range(entry.shape[0]):
                    acc[b * block_tiles + i] = acc[b * block_tiles + i] + terms[b]
                    if i < block_tiles - 1:
                        terms[b] = terms[b] * step
        gated = jnp.concatenate(acc, 0) * q_ref[:, cols].astype(F32)
        gated_ref[:, cols] = gated * gain_ref[:, cols]
        squares[...] = squares[...] + gated * gated
        return 0

    lax.fori_loop(0, q_ref.shape[1] // LANES, group_body, 0)
    high = squares[...].astype(BF16)
    low = (squares[...] - high.astype(F32)).astype(BF16)
    sums = lax.dot_general(
        jnp.ones((TILE, 2 * LANES), BF16), jnp.concatenate([high, low], 1), (((1,), (1,)), ((), ())),
        preferred_element_type=F32,
    )
    for i in range(sums_ref.shape[0]):
        sums_ref[i] = sums[0:1]


def shape(dims, dtype=F32):
    return jax.ShapeDtypeStruct(dims, dtype)


def call(kernel, name, out_shape, scratch, args, scalars=0, cost=None):
    vmem, smem = (pl.BlockSpec(memory_space=space) for space in (pltpu.VMEM, pltpu.SMEM))
    return pl.pallas_call(
        kernel,
        out_shape=out_shape,
        in_specs=[smem] * scalars + [vmem] * (len(args) - scalars),
        out_specs=jax.tree.map(lambda _: vmem, out_shape),
        scratch_shapes=[pltpu.VMEM(dims, F32) for dims in scratch],
        compiler_params=PARAMS,
        cost_estimate=cost,
        name=name,
    )(*args)


def cost(flops):
    return pl.CostEstimate(flops=int(flops), bytes_accessed=0, transcendentals=0)


def from_behind(block, axis):
    size = lax.axis_size(axis)
    return lax.ppermute(block, axis, [(i, (i + 1) % size) for i in range(size)])


def on_device(projected, short_filter, medium_filter, decay, residues, skip_gain, out_gain):
    _, rows, chans = projected.shape
    ctx, ch = lax.axis_size("ctx"), lax.axis_size("ch")
    index = lax.axis_index("ctx").reshape(1)
    short = jnp.pad(jnp.transpose(short_filter, (1, 0, 2)), ((0, 0), (0, TILE - SHORT), (0, 0)))
    edge, raw = call(
        edge_kernel, "edge", (shape((2, EDGE, chans), BF16), shape(projected.shape, BF16)), [], (projected,)
    )
    halo = from_behind(edge, "ctx")
    product, tail, head = call(
        feature_kernel,
        "features",
        (shape((rows, chans), BF16), shape((MED + EDGE, chans), BF16), shape((2, TILE, chans))),
        [(2, rows + TILE, LANES)],
        (raw, short),
        cost=cost(2e9),
    )
    tail = from_behind(tail, "ctx")
    partial = call(state_kernel, "states", shape((2, MODES, chans)), [], (product, decay), cost=cost(1e9))
    spread, first = call(
        functools.partial(first_kernel, row_count=rows),
        "first",
        (shape((ctx, MODES, chans), BF16), shape((TILE, chans))),
        [(chans // LANES, 2, 2 * TILE, LANES)],
        (index, halo, head, short, decay, partial),
        scalars=1,
        cost=cost(2e9),
    )
    states = lax.all_to_all(spread, "ctx", 0, 0, tiled=True)
    queries, base, spans, near, lead, out_gain = call(
        direct_kernel,
        "direct",
        (
            shape((rows, chans), BF16),
            shape((MODES * TILE, chans)),
            shape((3, MODES, chans)),
            shape((rows, chans)),
            shape((MED // BLOCK, MODES, chans)),
            shape((1, chans)),
        ),
        [
            (MED, LANES),
            (TILE, MED + BLOCK + TILE, LANES),
            (MED + rows, LANES),
            ((MED + rows) // 2, LANES),
            (rows + TILE, LANES),
        ],
        (index, medium_filter, decay, residues, skip_gain[None], out_gain[None], short, tail, raw, product, first),
        scalars=1,
        cost=cost(8e9),
    )
    gated, sums = call(
        combine_kernel,
        "combine",
        (shape((rows, chans)), shape((ch, 1, rows))),
        [(rows // BLOCK, MODES, chans), (rows, LANES)],
        (index, base, spans, states, lead, near, queries, out_gain),
        scalars=1,
    )
    sums = lax.all_to_all(sums, "ch", 0, 0, tiled=True)
    scale = lax.rsqrt(jnp.sum(sums, (0, 1)) / C + EPS)
    return (gated * scale[:, None]).astype(BF16)


def solution(mesh):
    in_specs = (
        P(None, "ctx", "ch"),
        P(None, None, "ch"),
        P(None, "ch"),
        P(None, "ch"),
        P(None, "ch"),
        P("ch"),
        P("ch"),
    )
    return jax.shard_map(on_device, mesh=mesh, in_specs=in_specs, out_specs=P("ctx", "ch"), check_vma=False)
```

```python
import functools
import jax
import jax.numpy as jnp
from jax import lax
from jax.experimental import pallas as pl
from jax.experimental.pallas import tpu as pltpu
from jax.sharding import PartitionSpec as P

C = 4096
SHORT = 7
MED = 128
MODES = 16
EPS = 1e-06
LANES = 128
TILE = 8
EDGE = 16
BLOCK = 64
F32 = jnp.float32
BF16 = jnp.bfloat16
PARAMS = pltpu.CompilerParams(vmem_limit_bytes=48 * 1024 * 1024)


def row_iota():
    return lax.broadcasted_iota(jnp.int32, (TILE, LANES), 0).astype(F32)


def lanes_of(group):
    return pl.ds(pl.multiple_of(group * LANES, LANES), LANES)


def one_minus_exp(x):
    return x * (1 - x * (1 / 2) * (1 - x * (1 / 3) * (1 - x * (1 / 4) * (1 - x * (1 / 5) * (1 - x * (1 / 6))))))


def tiles_of(array):
    return [array[TILE * i : TILE * (i + 1)] for i in range(array.shape[0] // TILE)]


def modal_sums(tiles, decay, rows):
    eight = jnp.exp(-TILE * decay)
    sums = []
    for n in range(MODES):
        step = jnp.broadcast_to(eight[n : n + 1], (TILE, LANES))
        state = tiles[0]
        for tile in tiles[1:]:
            state = state * step + tile
        sums.append(jnp.sum(state * jnp.exp(-decay[n : n + 1] * (TILE - 1 - rows)), axis=0, keepdims=True))
    return jnp.concatenate(sums, 0)


def short_sum(ext, taps, start, rows, first=0):
    total = 0.0
    for d in range(first, SHORT):
        total = total + taps[d : d + 1] * ext[start - d : start - d + rows]
    return total


def feature_kernel(raw_ref, short_ref, p_ref, tail_ref, head_ref, ext):
    row_count = raw_ref.shape[1]

    def group_body(group, _):
        cols = lanes_of(group)
        feats = []
        for j in range(2):
            ext[j, 0:TILE] = jnp.zeros((TILE, LANES), F32)
            ext[j, TILE:] = raw_ref[1 + j, :, cols].astype(F32)
            total = short_sum(ext.at[j], short_ref[1 + j, :, cols], TILE, row_count)
            head_ref[j, :, cols] = total[0:TILE]
            feats.append(total.astype(BF16).astype(F32))
        product = (feats[0] * feats[1]).astype(BF16)
        p_ref[:, cols] = product
        tail_ref[0:MED, cols] = product[row_count - MED :]
        tail_ref[MED:, cols] = raw_ref[0, row_count - EDGE :, cols]
        return 0

    lax.fori_loop(0, p_ref.shape[1] // LANES, group_body, 0)


def state_kernel(p_ref, decay_ref, sums_ref):
    part_tiles = (p_ref.shape[0] - MED) // TILE

    def group_body(group, _):
        cols = lanes_of(group)
        rows = row_iota()
        tiles = tiles_of(p_ref[:, cols].astype(F32))
        decay = decay_ref[:, cols]
        eight = jnp.exp(-TILE * decay)
        for n in range(MODES):
            step = jnp.broadcast_to(eight[n : n + 1], (TILE, LANES))
            close = jnp.exp(-decay[n : n + 1] * (TILE - 1 - rows))
            state = tiles[1]
            for i in range(2, len(tiles)):
                if i == part_tiles:
                    sums_ref[1, n : n + 1, cols] = jnp.sum(state * close, axis=0, keepdims=True)
                state = state * step + tiles[i]
            sums_ref[0, n : n + 1, cols] = jnp.sum(state * close, axis=0, keepdims=True)
        return 0

    lax.fori_loop(0, p_ref.shape[1] // LANES, group_body, 0)


def first_kernel(index_ref, halo_ref, head_ref, short_ref, decay_ref, sums_ref, spread_ref, first_ref, ext, *, row_count):
    following = jnp.minimum(index_ref[0] + 1, spread_ref.shape[0] - 1)

    def group_body(group, _):
        cols = lanes_of(group)
        feats = []
        for j in range(2):
            before = halo_ref[j, :, cols].astype(F32)[EDGE - TILE :]
            ext[group, j, 0:TILE] = jnp.where(index_ref[0] > 0, before, 0.0)
            ext[group, j, TILE:] = jnp.zeros((TILE, LANES), F32)
            total = head_ref[j, :, cols] + short_sum(ext.at[group, j], short_ref[1 + j, :, cols], TILE, TILE, 1)
            feats.append(total.astype(BF16).astype(F32))
        product = (feats[0] * feats[1]).astype(BF16).astype(F32)
        first_ref[:, cols] = product
        decay = decay_ref[:, cols]
        own = modal_sums([product], decay, row_iota())
        whole = sums_ref[0, :, cols] + own * jnp.exp(-float(row_count - TILE) * decay)
        part = sums_ref[1, :, cols] + own * jnp.exp(-float(row_count - MED - TILE) * decay)
        whole = whole.astype(BF16)
        for i in range(spread_ref.shape[0]):
            spread_ref[i, :, cols] = whole
        spread_ref[following, :, cols] = part.astype(BF16)
        return 0

    lax.fori_loop(0, spread_ref.shape[2] // LANES, group_body, 0, unroll=True)


def row_of(ref, row):
    return jnp.broadcast_to(ref[pl.ds(row, 1), :], (TILE, LANES))


def tile_at(bank, index):
    return bank[TILE * index : TILE * (index + 1)]


def pair_up(signal, pairs):
    half = BLOCK // 2
    for b in range(signal.shape[0] // BLOCK):
        pairs[half * b : half * (b + 1)] = signal[BLOCK * b : BLOCK * b + half] + signal[BLOCK * b + half : BLOCK * (b + 1)]


def no_sums(tiles):
    return tuple(jnp.zeros((TILE, LANES), F32) for _ in range(tiles + tiles // 2))


def with_pairs(acc, tiles):
    half = BLOCK // TILE // 2
    return [acc[i] + acc[tiles + i // (2 * half) * half + i % half] for i in range(tiles)]


def add_block(acc, tiles, out, block, distance, bank, signal, pairs, s):
    full = BLOCK // TILE
    half = full // 2
    base = full * distance
    reach = range(1 - half, half)
    mid = {o: tile_at(bank, base + o) for o in reach}
    upper = {o: tile_at(bank, base + o - half) - mid[o] for o in reach}
    lower = {o: tile_at(bank, base + o + half) - mid[o] for o in reach}
    for j in range(half):
        late = row_of(signal, TILE * (full * block + half + j) + s)
        early = row_of(signal, TILE * (full * block + j) + s)
        both = row_of(pairs, TILE * (half * block + j) + s)
        for i in range(half):
            at = full * out + i
            acc[at] = acc[at] + late * upper[i - j]
            acc[at + half] = acc[at + half] + early * lower[i - j]
            acc[tiles + half * out + i] = acc[tiles + half * out + i] + both * mid[i - j]


def direct_kernel(index_ref, med_ref, decay_ref, res_ref, skip_ref, gain_ref, short_ref, tail_ref, raw_ref, p_ref, first_ref,
                  q_ref, base_ref, spans_ref, near_ref, sums_ref, held_ref, med_f32, shifted, signal, pairs, ext):
    row_count = p_ref.shape[0]
    out_tiles = row_count // TILE
    block_tiles = BLOCK // TILE
    blocks = sums_ref.shape[0]
    med_tiles = MED // TILE
    far_tiles = BLOCK // TILE
    reach = MED + BLOCK
    held_ref[...] = gain_ref[...]

    def group_body(group, _):
        cols = lanes_of(group)
        rows = row_iota()
        decay = decay_ref[:, cols]
        weights = res_ref[:, cols] * jnp.sqrt(one_minus_exp(2.0 * decay))
        eight = jnp.exp(-TILE * decay)
        spans_ref[0, :, cols] = jnp.exp(-float(row_count) * decay)
        spans_ref[1, :, cols] = jnp.exp(-float(BLOCK) * decay)
        spans_ref[2, :, cols] = eight
        med = med_ref[:, cols].astype(F32)
        med_f32[...] = med
        near = [jnp.zeros((TILE, LANES), F32) for _ in range(med_tiles)]
        far = [jnp.zeros((TILE, LANES), F32) for _ in range(far_tiles)]
        for n in range(MODES):
            rate = decay[n : n + 1]
            step = jnp.broadcast_to(eight[n : n + 1], (TILE, LANES))
            weight = weights[n : n + 1]
            term = weight * jnp.exp(-rate * rows)
            state = jnp.zeros((TILE, LANES), F32)
            for i in range(med_tiles):
                near[i] = near[i] + term
                term = term * step
                state = state * step + med[TILE * i : TILE * (i + 1)]
            reach_weight = jnp.sum(state * jnp.exp(-rate * (TILE - 1 - rows)), axis=0, keepdims=True) * weight
            base_ref[TILE * n : TILE * (n + 1), cols] = reach_weight * jnp.exp(-rate * (rows + 2))
            term = reach_weight * jnp.exp(-rate * (rows + 1))
            for i in range(far_tiles):
                far[i] = far[i] + term
                term = term * step
        near[0] = near[0] + jnp.where(rows == 0, skip_ref[:, cols], 0.0)
        taps = jnp.concatenate(near, 0)
        for s in range(TILE):
            shifted[s, 0:TILE] = jnp.zeros((TILE, LANES), F32)
            shifted[s, s : s + MED] = taps

        def taps_body(s, acc):
            acc = list(acc)
            bank = [shifted[s, TILE * i : TILE * (i + 1)] for i in range(med_tiles)]
            for j in range(med_tiles):
                row = jnp.broadcast_to(med_f32[pl.ds(TILE * j + s, 1), :], (TILE, LANES))
                for i in range(j, med_tiles):
                    acc[i] = acc[i] + row * bank[i - j]
            return tuple(acc)

        acc = lax.fori_loop(0, TILE, taps_body, tuple(jnp.zeros((TILE, LANES), F32) for _ in range(med_tiles)))
        taps = jnp.concatenate(list(acc) + far, 0)
        for s in range(TILE):
            shifted[s, 0:TILE] = jnp.zeros((TILE, LANES), F32)
            shifted[s, s : s + reach] = taps
        tail = jnp.where(index_ref[0] > 0, tail_ref[:, cols].astype(F32), 0.0)
        lead = tail[0:MED]
        ext[0:TILE] = tail[MED + EDGE - TILE :]
        ext[TILE:] = raw_ref[0, :, cols].astype(F32)
        q_ref[:, cols] = short_sum(ext, short_ref[0, :, cols], TILE, row_count).astype(BF16)
        signal[0:MED] = lead
        signal[MED : MED + row_count] = p_ref[:, cols].astype(F32)
        signal[MED : MED + TILE] = first_ref[:, cols]
        for b in range(blocks):
            tiles = tiles_of(lead[BLOCK * b : BLOCK * (b + 1)])
            sums_ref[b, :, cols] = modal_sums(tiles, decay, rows)

        pair_up(signal, pairs)

        def direct_body(s, acc):
            bank = shifted.at[s]
            acc = list(acc)
            for j in range(out_tiles):
                row = row_of(signal, MED + TILE * j + s)
                for i in range(j, (j // block_tiles + 1) * block_tiles):
                    acc[i] = acc[i] + row * tile_at(bank, i - j)
            for out in range(out_tiles // block_tiles):
                for distance in range(1, blocks + 1):
                    add_block(acc, out_tiles, out, out + blocks - distance, distance, bank, signal, pairs, s)
            return tuple(acc)

        acc = lax.fori_loop(0, TILE, direct_body, no_sums(out_tiles))
        near_ref[:, cols] = jnp.concatenate(with_pairs(acc, out_tiles), 0)
        return 0

    lax.fori_loop(0, p_ref.shape[1] // LANES, group_body, 0)


def combine_kernel(index_ref, base_ref, spans_ref, states_ref, lead_ref, near_ref, q_ref, gain_ref,
                   gated_ref, sums_ref, entry, squares):
    block_tiles = BLOCK // TILE
    own = index_ref[0]
    squares[...] = jnp.zeros(squares.shape, F32)
    span, block_span = spans_ref[0], spans_ref[1]

    def carry_body(j, carried):
        return carried * span + states_ref[j].astype(F32)

    carried = lax.fori_loop(0, own - 1, carry_body, jnp.zeros(span.shape, F32))
    part = states_ref[jnp.maximum(own - 1, 0)].astype(F32)
    state = jnp.where(own > 0, part, 0.0) + block_span * carried
    for b in range(entry.shape[0]):
        entry[b] = state
        if b < lead_ref.shape[0]:
            state = state * block_span + lead_ref[b]

    def group_body(group, _):
        cols = lanes_of(group)
        eight = spans_ref[2, :, cols]
        acc = tiles_of(near_ref[:, cols])
        for n in range(MODES):
            step = jnp.broadcast_to(eight[n : n + 1], (TILE, LANES))
            base = base_ref[TILE * n : TILE * (n + 1), cols]
            terms = [entry[b, n : n + 1, cols] * base for b in range(entry.shape[0])]
            for i in range(block_tiles):
                for b in range(entry.shape[0]):
                    acc[b * block_tiles + i] = acc[b * block_tiles + i] + terms[b]
                    if i < block_tiles - 1:
                        terms[b] = terms[b] * step
        gated = jnp.concatenate(acc, 0) * q_ref[:, cols].astype(F32)
        gated_ref[:, cols] = gated * gain_ref[:, cols]
        squares[...] = squares[...] + gated * gated
        return 0

    lax.fori_loop(0, q_ref.shape[1] // LANES, group_body, 0)
    high = squares[...].astype(BF16)
    low = (squares[...] - high.astype(F32)).astype(BF16)
    sums = lax.dot_general(
        jnp.ones((TILE, 2 * LANES), BF16), jnp.concatenate([high, low], 1), (((1,), (1,)), ((), ())),
        preferred_element_type=F32,
    )
    for i in range(sums_ref.shape[0]):
        sums_ref[i] = sums[0:1]


def shape(dims, dtype=F32):
    return jax.ShapeDtypeStruct(dims, dtype)


def call(kernel, name, out_shape, scratch, args, scalars=0, cost=None):
    vmem, smem = (pl.BlockSpec(memory_space=space) for space in (pltpu.VMEM, pltpu.SMEM))
    return pl.pallas_call(
        kernel,
        out_shape=out_shape,
        in_specs=[smem] * scalars + [vmem] * (len(args) - scalars),
        out_specs=jax.tree.map(lambda _: vmem, out_shape),
        scratch_shapes=[pltpu.VMEM(dims, F32) for dims in scratch],
        compiler_params=PARAMS,
        cost_estimate=cost,
        name=name,
    )(*args)


def cost(flops):
    return pl.CostEstimate(flops=int(flops), bytes_accessed=0, transcendentals=0)


def from_behind(block, axis):
    size = lax.axis_size(axis)
    return lax.ppermute(block, axis, [(i, (i + 1) % size) for i in range(size)])


def on_device(projected, short_filter, medium_filter, decay, residues, skip_gain, out_gain):
    _, rows, chans = projected.shape
    ctx, ch = lax.axis_size("ctx"), lax.axis_size("ch")
    index = lax.axis_index("ctx").reshape(1)
    short = jnp.pad(jnp.transpose(short_filter, (1, 0, 2)), ((0, 0), (0, TILE - SHORT), (0, 0)))
    raw = projected
    edge = projected[1:, rows - EDGE :]
    halo = from_behind(edge, "ctx")
    product, tail, head = call(
        feature_kernel,
        "features",
        (shape((rows, chans), BF16), shape((MED + EDGE, chans), BF16), shape((2, TILE, chans))),
        [(2, rows + TILE, LANES)],
        (raw, short),
        cost=cost(2e9),
    )
    tail = from_behind(tail, "ctx")
    partial = call(state_kernel, "states", shape((2, MODES, chans)), [], (product, decay), cost=cost(1e9))
    spread, first = call(
        functools.partial(first_kernel, row_count=rows),
        "first",
        (shape((ctx, MODES, chans), BF16), shape((TILE, chans))),
        [(chans // LANES, 2, 2 * TILE, LANES)],
        (index, halo, head, short, decay, partial),
        scalars=1,
        cost=cost(2e9),
    )
    states = lax.all_to_all(spread, "ctx", 0, 0, tiled=True)
    queries, base, spans, near, lead, out_gain = call(
        direct_kernel,
        "direct",
        (
            shape((rows, chans), BF16),
            shape((MODES * TILE, chans)),
            shape((3, MODES, chans)),
            shape((rows, chans)),
            shape((MED // BLOCK, MODES, chans)),
            shape((1, chans)),
        ),
        [
            (MED, LANES),
            (TILE, MED + BLOCK + TILE, LANES),
            (MED + rows, LANES),
            ((MED + rows) // 2, LANES),
            (rows + TILE, LANES),
        ],
        (index, medium_filter, decay, residues, skip_gain[None], out_gain[None], short, tail, raw, product, first),
        scalars=1,
        cost=cost(8e9),
    )
    gated, sums = call(
        combine_kernel,
        "combine",
        (shape((rows, chans)), shape((ch, 1, rows))),
        [(rows // BLOCK, MODES, chans), (rows, LANES)],
        (index, base, spans, states, lead, near, queries, out_gain),
        scalars=1,
    )
    sums = lax.all_to_all(sums, "ch", 0, 0, tiled=True)
    scale = lax.rsqrt(jnp.sum(sums, (0, 1)) / C + EPS)
    return (gated * scale[:, None]).astype(BF16)


def solution(mesh):
    in_specs = (
        P(None, "ctx", "ch"),
        P(None, None, "ch"),
        P(None, "ch"),
        P(None, "ch"),
        P(None, "ch"),
        P("ch"),
        P("ch"),
    )
    return jax.shard_map(on_device, mesh=mesh, in_specs=in_specs, out_specs=P("ctx", "ch"), check_vma=False)
```
